32 devices in a mesh: groups: 2 (over y), expert: 16 (over z, x, core), dp: 1.
Axes of the slice: x: 2, y: 2, z: 4, core: 2. Of those that a mesh axis runs over, the one named last changes fastest.
Arguments:
- hidden_saved: bfloat16 [4096, 8, 768], P(('groups', 'expert', 'dp')), parts along dimension 0, may hold values from -4.6 to 4.6
- grad_out: bfloat16 [4096, 2048], P(('groups', 'expert', 'dp')), parts along dimension 0, may hold values from -4.6 to 4.6
- expert_ids: int32 [4096, 8], P(('groups', 'expert', 'dp')), parts along dimension 0, may hold values from 0 to 15, all different within a row; in each aligned block of 128 rows (0 to 127, 128 to 255, ...) at most 128 rows name the same one
- gate_codes: int32 [4096, 8], P(('groups', 'expert', 'dp')), parts along dimension 0, may hold values from 64 to 255
- clip_bound: float32 [128], P(('groups', 'expert', 'dp')), parts along dimension 0, may hold values from 1605.2976 to 9029.799
Outputs:
- grad_down: bfloat16 [32, 2048, 768], P(('groups', 'expert'), 'dp'), parts along dimension 0
- clip_factors: float32 [128], P(('groups', 'expert', 'dp')), parts along dimension 0
The draws below stay inside these ranges and needn't reach their ends.
There are 2 independent parts, one for each index of `groups`. The reference program is written for one: setup_inputs(seed, part) draws one part's arguments, and reference() takes and returns one part's arrays. A program takes and returns all parts, laid end to end along the dimension named above; each array names one. Nothing has to cross between parts.
Inputs may be any that keep to these rules, and one draw needn't show every extreme that they name: `expert_ids`: each row names 8 different experts. Among the 128 rows of one device no expert is named more than 128 times, a bound that some block reaches.
All inputs are finite; a program needn't handle non-finite values.
Results may differ from the reference program's by a relative error of at most 0.011.
Values may be sent and summed in bfloat16 or wider, within the bound.
No kernel may reach another device: no remote copies, remote signals or barrier semaphores. Data moves between devices by JAX's collectives and lax.ppermute only.
A program may use at most 128 MiB of HBM per device.

```python
import math
import jax
import jax.numpy as jnp
import numpy as np
from jax import lax

D = 2048
HID = 768
TOPK = 8
EXLEN = 32
EXPERTS = 16
TOK_DEV = 128
MOST = 128
TOKENS = 2048
EXAMPLES = 64
N_EXPERT = 16
N_DP = 1


def draw_hidden_saved(key, part):
    key = jax.random.fold_in(key, 11)
    key_noise, key_direction, key_sign = jax.random.split(key, 3)
    noise = jnp.clip(jax.random.normal(key_noise, (TOKENS, TOPK, HID), jnp.float32), -4.0, 4.0)
    amplitude = 0.55
    direction = jax.random.rademacher(key_direction, (HID,), jnp.float32)
    signs = jnp.repeat(jax.random.rademacher(key_sign, (TOKENS // EXLEN,), jnp.float32), EXLEN)
    values = noise + amplitude * signs[:, None, None] * direction[None, None, :]
    return values.astype(jnp.bfloat16)


def draw_grad_out(key, part):
    key = jax.random.fold_in(key, 23)
    key_noise, key_direction, key_sign = jax.random.split(key, 3)
    noise = jnp.clip(jax.random.normal(key_noise, (TOKENS, D), jnp.float32), -4.0, 4.0)
    amplitude = 0.55
    direction = jax.random.rademacher(key_direction, (D,), jnp.float32)
    signs = jnp.repeat(jax.random.rademacher(key_sign, (TOKENS // EXLEN,), jnp.float32), EXLEN)
    values = noise + amplitude * signs[:, None] * direction[None, :]
    return values.astype(jnp.bfloat16)


def touch_ends(result, rng, low, high):
    extent = result.shape
    place = [jax.random.randint(jax.random.fold_in(rng, axis), (), 0, extent[axis]) for axis in range(len(extent))]
    result = result.at[tuple(place)].set(low)
    longest = extent.index(max(extent))
    place[longest] = (place[longest] + 1) % extent[longest]
    return result.at[tuple(place)].set(high)


def block_levels(rng, extent, pieces, smallest, top_value):
    def one(dim, parts):
        heights = jax.random.uniform(jax.random.fold_in(jax.random.fold_in(rng, 6), dim), (parts,), jnp.float32, smallest / len(pieces), top_value / len(pieces))
        return jnp.repeat(jnp.exp(heights), extent[dim] // parts).reshape((-1,) + (1,) * (len(extent) - dim - 1))

    loudness = one(*pieces[0])
    for cut in pieces[1:]:
        loudness = loudness * one(*cut)
    return loudness


def assign_block(own_key, own, number, rows, amount, top, most, lean):
    sequence = jax.random.permutation(own_key, amount)
    crowded, ordinary = load_shares(amount, rows * top, most, lean, True), load_shares(amount, rows * top, most, lean, False)
    places = jnp.arange(amount)

    def named(lengths, offset_by):
        used = int((lengths > 0).sum())
        fixed = max(1, used // 4)
        passed = fixed + (places - fixed + offset_by * (used - fixed)) % max(1, amount - fixed)
        return jnp.zeros((amount,), jnp.int32).at[sequence[jnp.where(places < fixed, places, passed)]].set(jnp.asarray(lengths, jnp.int32))

    lengths = jnp.where(number % 4 == 0, named(crowded, number // 4), named(ordinary, number - number // 4 - 1))
    mixed = jax.random.permutation(jax.random.fold_in(own, 3), amount)
    donor, receiver = mixed[0:amount // 2 * 2:2], mixed[1:amount // 2 * 2:2]
    slack = jnp.minimum(lengths[donor] - 1, most - lengths[receiver]) // 2
    slack = jnp.where((donor == sequence[0]) | (receiver == sequence[0]) | (lengths[receiver] == 0), 0, jnp.maximum(slack, 0))
    passed = jax.random.randint(jax.random.fold_in(own, 4), (amount // 2,), 0, 1 << 20) % (slack + 1)
    lengths = lengths.at[donor].add(-passed).at[receiver].add(passed)
    items = jnp.searchsorted(jnp.cumsum(lengths), jnp.arange(rows * top), side="right").astype(jnp.int32)
    grid = items.reshape(top, rows).T
    grid = grid[jax.random.permutation(jax.random.fold_in(own, 1), rows)]
    offset_by = jax.random.randint(jax.random.fold_in(own, 2), (rows, 1), 0, top)
    return jnp.take_along_axis(grid, (jnp.arange(top)[None, :] + offset_by) % top, axis=1)


def load_shares(count, total, reach, skew, full):
    loads = [(1 << 20) // math.isqrt(standing ** skew) + 1 for standing in range(1, count + 1)]
    largest = reach if full else min(reach, max(-(-total // count), total * loads[0] // sum(loads)))
    least = 1 if total - largest >= count - 1 else 0
    counts, spare = [largest] + [least] * (count - 1), total - largest - least * (count - 1)
    while spare > 0:
        free = [i for i in range(1, count) if counts[i] < largest] or [i for i in range(1, count) if counts[i] < reach]
        whole, left = sum([loads[i] for i in free]), spare
        for i in free:
            more = min(reach - counts[i], max(1, left * loads[i] // whole), spare)
            counts[i] = counts[i] + more
            spare = spare - more
    return np.array(counts)


def setup_inputs(seed: int = 0, part: int = 0) -> dict:
    keys = jax.random.split(jax.random.key(seed), 6)
    part_splits = jax.random.split(jax.random.fold_in(keys[5], part), 6)
    hidden_saved = draw_hidden_saved(jax.random.fold_in(jax.random.fold_in(keys[5], part), 71), part)
    grad_out = draw_grad_out(jax.random.fold_in(jax.random.fold_in(keys[5], part), 71), part)
    expert_ids_keys = jax.random.split(jax.random.fold_in(part_splits[2], 1), TOKENS // TOK_DEV)
    expert_ids_turns = jax.random.permutation(jax.random.fold_in(part_splits[2], 3), TOKENS // TOK_DEV)
    expert_ids = jax.vmap(lambda own, number: assign_block(jax.random.fold_in(part_splits[2], 2), own, number, TOK_DEV, EXPERTS, TOPK, MOST, 2))(expert_ids_keys, expert_ids_turns).reshape((TOKENS, TOPK))
    gate_codes = touch_ends(jax.random.randint(part_splits[3], (TOKENS, TOPK), 64, 256), jax.random.fold_in(part_splits[3], 1), 64, 255).astype(jnp.int32)
    clip_bound = jnp.clip(jnp.exp(math.log(9029.799) - 1.7272209 * jax.random.uniform(part_splits[4], (EXAMPLES,), jnp.float32) ** block_levels(part_splits[4], (EXAMPLES,), ((0, 16),), -0.2, 0.2)), 1605.2976, 9029.799)
    return dict(hidden_saved=hidden_saved, grad_out=grad_out, expert_ids=expert_ids, gate_codes=gate_codes, clip_bound=clip_bound)


def ghost_norm(args):
    hidden, grad_rows, expert_row, gate_row = args
    hid_gram = jnp.dot(hidden, hidden.T, preferred_element_type=jnp.float32)
    grad_gram = jnp.dot(grad_rows, grad_rows.T, preferred_element_type=jnp.float32)
    grad_pairs = jnp.repeat(jnp.repeat(grad_gram, TOPK, axis=0), TOPK, axis=1)
    same_expert = (expert_row[:, None] == expert_row[None, :]).astype(jnp.float32)
    return jnp.sum(hid_gram * grad_pairs * same_expert * gate_row[:, None] * gate_row[None, :])

def slot_numbers(ids_block):
    onehot = (ids_block[:, None] == jnp.arange(EXPERTS, dtype=jnp.int32)[None, :]).astype(jnp.int32)
    return (lax.optimization_barrier(jnp.sum(jnp.cumsum(onehot, axis=0) * onehot, axis=1)) - 1).astype(jnp.int32)

def reference(hidden_saved, grad_out, expert_ids, gate_codes, clip_bound):
    blocks = N_EXPERT * N_DP
    per_block = TOK_DEV * TOPK
    gate_values = gate_codes.astype(jnp.float32) / 1024.0
    norm_values = lax.map(ghost_norm, (hidden_saved.reshape(EXAMPLES, EXLEN * TOPK, HID), grad_out.reshape(EXAMPLES, EXLEN, D), expert_ids.reshape(EXAMPLES, EXLEN * TOPK), gate_values.reshape(EXAMPLES, EXLEN * TOPK)))
    clip_factors = jnp.minimum(1.0, clip_bound / jnp.sqrt(norm_values + 1e-06))
    pair_scale = jnp.repeat(clip_factors, EXLEN * TOPK) * gate_values.reshape(-1)
    ids_blocks = expert_ids.reshape(blocks, per_block)
    slot_ids = lax.map(slot_numbers, ids_blocks)
    block_index = jnp.arange(blocks, dtype=jnp.int32)
    sentinel = blocks * per_block
    slot_table = jnp.full((N_DP, EXPERTS, N_EXPERT, MOST), sentinel, dtype=jnp.int32)
    slot_table = slot_table.at[(block_index % N_DP)[:, None], ids_blocks, (block_index // N_DP)[:, None], slot_ids].set(jnp.arange(sentinel, dtype=jnp.int32).reshape(blocks, per_block))
    hidden_rows = jnp.concatenate([hidden_saved.reshape(sentinel, HID), jnp.zeros((1, HID), jnp.bfloat16)], axis=0)
    grad_rows = jnp.concatenate([grad_out, jnp.zeros((1, D), jnp.bfloat16)], axis=0)
    scale_rows = jnp.concatenate([pair_scale, jnp.zeros((1,), jnp.float32)], axis=0)

    def per_expert(expert):
        accum_total = jnp.zeros((D, HID), jnp.float32)
        for group_half in range(N_DP):
            row_index = slot_table[group_half, expert].reshape(-1)
            hidden = hidden_rows[row_index].astype(jnp.float32)
            scaled = (scale_rows[row_index][:, None] * grad_rows[row_index // TOPK].astype(jnp.float32)).astype(jnp.bfloat16)
            scaled = lax.optimization_barrier(scaled).astype(jnp.float32)
            term_block = jnp.dot(scaled.T, hidden, precision=lax.Precision.HIGHEST).astype(jnp.bfloat16)
            accum_total = accum_total + lax.optimization_barrier(term_block).astype(jnp.float32)
        return accum_total.astype(jnp.bfloat16)
    grad_down = lax.map(per_expert, jnp.arange(EXPERTS, dtype=jnp.int32))
    return (grad_down, clip_factors)
```

```python
import functools

import jax
import jax.numpy as jnp
import numpy as np
from jax import lax
from jax.experimental import pallas as pl
from jax.experimental.pallas import tpu as pltpu
from jax.sharding import PartitionSpec as P

TOPK = 8
EXLEN = 32
VMEM_LIMIT = 56 * 1024 * 1024
HIGHEST = lax.Precision.HIGHEST


def per_device_sparse(hidden_saved, grad_out, expert_ids, gate_codes, clip_bound):
    experts = lax.axis_size("expert")
    tokens_dev = grad_out.shape[0]
    width = grad_out.shape[1]
    hidden_width = hidden_saved.shape[2]
    examples_dev = clip_bound.shape[0]
    count_pairs = tokens_dev * TOPK
    capacity = min(tokens_dev, 2 * tokens_dev * TOPK // experts)
    ids_flat = expert_ids.reshape(count_pairs)
    onehot = (ids_flat[:, None] == jnp.arange(experts, dtype=jnp.int32)[None, :]).astype(jnp.int32)
    slot_ids = jnp.sum(jnp.cumsum(onehot, axis=0) * onehot, axis=1) - 1
    target = ids_flat * capacity + slot_ids
    hid_rows = hidden_saved.reshape(count_pairs, hidden_width)
    h_buffer = jnp.zeros((experts * capacity, hidden_width), jnp.bfloat16).at[target].set(hid_rows)
    h_buffer = h_buffer.reshape(experts, capacity, hidden_width)
    dy_pairs = jnp.repeat(grad_out, TOPK, axis=0)
    dy_buffer = jnp.zeros((experts * capacity, width), jnp.bfloat16).at[target].set(dy_pairs)
    dy_buffer = dy_buffer.reshape(experts, capacity, width)
    pair_info = jnp.stack(
        [
            gate_codes.reshape(count_pairs),
            jnp.arange(count_pairs, dtype=jnp.int32) // (EXLEN * TOPK),
        ],
        axis=1,
    ).astype(jnp.bfloat16)
    info_buffer = jnp.zeros((experts * capacity, 2), jnp.bfloat16).at[target].set(pair_info)
    info_buffer = info_buffer.reshape(experts, capacity, 2)
    recv_hidden, recv_dy, recv_info = (
        lax.all_to_all(h_buffer, "expert", split_axis=0, concat_axis=0, tiled=True),
        lax.all_to_all(dy_buffer, "expert", split_axis=0, concat_axis=0, tiled=True),
        lax.all_to_all(info_buffer, "expert", split_axis=0, concat_axis=0, tiled=True),
    )
    gate_recv = recv_info[:, :, 0].astype(jnp.float32) / 1024.0
    example_recv = recv_info[:, :, 1].astype(jnp.float32)
    owner_mask = (
        example_recv[:, :, None] == jnp.arange(examples_dev, dtype=jnp.float32)[None, None, :]
    ).astype(jnp.float32)
    hid_gram = jnp.einsum(
        "smh,snh->smn", recv_hidden, recv_hidden, preferred_element_type=jnp.float32
    )
    grad_gram = jnp.einsum("smd,snd->smn", recv_dy, recv_dy, preferred_element_type=jnp.float32)
    weights = hid_gram * grad_gram * gate_recv[:, :, None] * gate_recv[:, None, :]
    partial_value = jnp.sum(jnp.einsum("smn,snx->smx", weights, owner_mask) * owner_mask, axis=1)
    bounds_all = lax.all_gather(clip_bound, "expert", axis=0, tiled=True).reshape(
        experts, examples_dev
    )
    totals = lax.psum(partial_value, "expert")
    factor_all = jnp.minimum(1.0, bounds_all / jnp.sqrt(totals + 1e-06))
    factors = lax.dynamic_index_in_dim(factor_all, lax.axis_index("expert"), 0, keepdims=False)
    pair_scale = jnp.sum(owner_mask * factor_all[:, None, :], axis=2) * gate_recv
    recv_scaled = (pair_scale[:, :, None] * recv_dy.astype(jnp.float32)).astype(jnp.bfloat16)
    summed = lax.psum_scatter(
        lax.dot_general(
            recv_scaled,
            recv_hidden,
            (((0, 1), (0, 1)), ((), ())),
            preferred_element_type=jnp.float32,
        ).astype(jnp.bfloat16),
        "dp",
        scatter_dimension=0,
        tiled=True,
    )
    return (summed[None], factors)


def norm_kernel(experts, dy_ref, hid_ref, ids_ref, gate_ref, bound_ref, meta_ref, factor_ref):
    examples = ids_ref.shape[0]
    pairs = EXLEN * TOPK
    spread = (
        lax.broadcasted_iota(jnp.int32, (pairs, EXLEN), 0) // TOPK
        == lax.broadcasted_iota(jnp.int32, (pairs, EXLEN), 1)
    ).astype(jnp.float32)
    for x in range(examples):
        ids_row = ids_ref[x : x + 1, :]
        gate_row = gate_ref[x : x + 1, :].astype(jnp.float32) / 1024.0
        hid = hid_ref[x * pairs : (x + 1) * pairs, :]
        dy = dy_ref[x * EXLEN : (x + 1) * EXLEN, :]
        hid_gram = lax.dot_general(hid, hid, (((1,), (1,)), ((), ())), preferred_element_type=jnp.float32)
        dy_gram = lax.dot_general(dy, dy, (((1,), (1,)), ((), ())), preferred_element_type=jnp.float32)
        half = jnp.dot(spread, dy_gram, precision=HIGHEST, preferred_element_type=jnp.float32)
        pair_gram = lax.dot_general(
            half, spread, (((1,), (1,)), ((), ())), precision=HIGHEST, preferred_element_type=jnp.float32
        )
        onehot = (lax.broadcasted_iota(jnp.int32, (experts, pairs), 0) == ids_row).astype(jnp.float32)
        same = lax.dot_general(onehot, onehot, (((0,), (0,)), ((), ())), preferred_element_type=jnp.float32)
        weights = hid_gram * pair_gram * same
        sums = jnp.dot(gate_row, weights, precision=HIGHEST, preferred_element_type=jnp.float32)
        norm = jnp.sum(sums * gate_row, axis=1, keepdims=True)
        factor = jnp.minimum(1.0, bound_ref[x : x + 1, :] / jnp.sqrt(norm + 1e-06))
        factor_ref[x : x + 1, :] = factor
        meta_ref[x : x + 1, :] = factor * gate_row
        meta_ref[examples + x : examples + x + 1, :] = ids_row.astype(jnp.float32)


def build_kernel(chips, place_ref, own_ref, sib_ref, own_meta_ref, sib_meta_ref, *out_refs):
    examples = own_meta_ref.shape[0] // 2
    pairs = EXLEN * TOPK
    rows = chips * EXLEN
    me = place_ref[0]
    row = lax.broadcasted_iota(jnp.int32, (rows, pairs), 0)
    lane = lax.broadcasted_iota(jnp.int32, (rows, pairs), 1)
    same_token = (row % EXLEN) == (lane // TOPK)
    expert = (lax.bitwise_xor(row // EXLEN, me // 2) * 2 + me % 2).astype(jnp.float32)
    for side, (hid_ref, meta_ref) in enumerate(((own_ref, own_meta_ref), (sib_ref, sib_meta_ref))):
        for x in range(examples):
            hit = same_token & (meta_ref[examples + x : examples + x + 1, :] == expert)
            scale = jnp.sum(jnp.where(hit, meta_ref[x : x + 1, :], 0.0), axis=1, keepdims=True)
            picked = jnp.dot(
                hit.astype(jnp.float32).astype(jnp.bfloat16),
                hid_ref[x * pairs : (x + 1) * pairs, :],
                preferred_element_type=jnp.float32,
            )
            message = (picked * scale).astype(jnp.bfloat16)
            start = (side * examples + x) * EXLEN
            for j in range(chips):
                out_refs[j][start : start + EXLEN, :] = message[j * EXLEN : (j + 1) * EXLEN, :]


def product_kernel(chips, tokens, pos_ref, own_ref, sib_ref, *refs):
    hid_refs, out_ref = refs[:chips], refs[chips]
    total = None
    for j in range(chips):
        begin = pl.multiple_of(pos_ref[j] * tokens, tokens)
        dy = jnp.concatenate([own_ref[pl.ds(begin, tokens), :], sib_ref[pl.ds(begin, tokens), :]], axis=0)
        term = lax.dot_general(
            dy, hid_refs[j][...], (((0,), (0,)), ((), ())), preferred_element_type=jnp.float32
        )
        total = term if total is None else total + term
    out_ref[...] = total.astype(jnp.bfloat16)


def per_device_dense(hidden_saved, grad_out, expert_ids, gate_codes, clip_bound):
    devices = lax.axis_size("expert")
    chips = devices // 2
    tokens, width = grad_out.shape
    hidden = hidden_saved.shape[2]
    examples = clip_bound.shape[0]
    pairs = EXLEN * TOPK
    me = lax.axis_index("expert")
    ring = list(range(0, chips, 2)) + list(range(chips - 1, 0, -2))
    params = pltpu.CompilerParams(vmem_limit_bytes=VMEM_LIMIT)

    def swap(array, offset):
        return lax.ppermute(array, "expert", [(i, i ^ offset) for i in range(devices)])

    own_dy = lax.all_gather(
        grad_out,
        "expert",
        axis=0,
        tiled=True,
        axis_index_groups=[[2 * chip + core for chip in ring] for core in range(2)],
    )
    hid_rows = hidden_saved.reshape(tokens * TOPK, hidden)
    sib_rows = swap(hid_rows, 1)
    meta, factors = pl.pallas_call(
        functools.partial(norm_kernel, devices),
        out_shape=(
            jax.ShapeDtypeStruct((2 * examples, pairs), jnp.float32),
            jax.ShapeDtypeStruct((examples, 1), jnp.float32),
        ),
        compiler_params=params,
        name="norms",
    )(
        grad_out,
        hid_rows,
        expert_ids.reshape(examples, pairs),
        gate_codes.reshape(examples, pairs),
        clip_bound.reshape(examples, 1),
    )
    sib_meta = swap(meta, 1)
    messages = pl.pallas_call(
        functools.partial(build_kernel, chips),
        out_shape=[jax.ShapeDtypeStruct((2 * tokens, hidden), jnp.bfloat16)] * chips,
        in_specs=[pl.BlockSpec(memory_space=pltpu.SMEM)] + [pl.BlockSpec(memory_space=pltpu.VMEM)] * 4,
        compiler_params=params,
        name="build",
    )(me.astype(jnp.int32).reshape(1), hid_rows, sib_rows, meta, sib_meta)
    order = sorted(range(1, chips), key=lambda j: (-(j // 4 > 0), j))
    slots = {0: messages[0]}
    for j in order:
        slots[j] = swap(messages[j], 2 * j)
    own_dy = lax.optimization_barrier((own_dy, slots[order[0]]))[0]
    sib_dy = swap(own_dy, 1)
    where = np.argsort(np.array(ring)).astype(np.int32)
    position = jnp.asarray(where)[jnp.arange(chips, dtype=jnp.int32) ^ (me // 2)]
    block = 256
    summed = pl.pallas_call(
        functools.partial(product_kernel, chips, tokens),
        out_shape=jax.ShapeDtypeStruct((width, hidden), jnp.bfloat16),
        grid_spec=pltpu.PrefetchScalarGridSpec(
            num_scalar_prefetch=1,
            grid=(width // block,),
            in_specs=[pl.BlockSpec((chips * tokens, block), lambda i, pos: (0, i))] * 2
            + [pl.BlockSpec((2 * tokens, hidden), lambda i, pos: (0, 0))] * chips,
            out_specs=pl.BlockSpec((block, hidden), lambda i, pos: (i, 0)),
        ),
        compiler_params=params,
        name="product",
    )(position, own_dy, sib_dy, *[slots[j] for j in range(chips)])
    return (summed[None], factors.reshape(examples))


def solution(mesh):
    def per_device(hidden_saved, grad_out, expert_ids, gate_codes, clip_bound):
        devices = mesh.shape["expert"]
        tokens = grad_out.shape[0]
        dense = (
            mesh.shape["dp"] == 1
            and devices >= 4
            and devices & (devices - 1) == 0
            and 2 * tokens * TOPK // devices >= tokens
        )
        run = per_device_dense if dense else per_device_sparse
        return run(hidden_saved, grad_out, expert_ids, gate_codes, clip_bound)

    return jax.shard_map(
        per_device,
        mesh=mesh,
        in_specs=(
            P(("groups", "expert", "dp"), None, None),
            P(("groups", "expert", "dp"), None),
            P(("groups", "expert", "dp"), None),
            P(("groups", "expert", "dp"), None),
            P(("groups", "expert", "dp")),
        ),
        out_specs=(P(("groups", "expert"), "dp", None), P(("groups", "expert", "dp"))),
        check_vma=False,
    )
```

```python
import functools

import jax
import jax.numpy as jnp
from jax import lax
from jax.experimental import pallas as pl
from jax.experimental.pallas import tpu as pltpu
from jax.sharding import PartitionSpec as P

TOPK = 8
EXLEN = 32
VMEM_LIMIT = 56 * 1024 * 1024
HIGHEST = lax.Precision.HIGHEST


def per_device_sparse(hidden_saved, grad_out, expert_ids, gate_codes, clip_bound):
    experts = lax.axis_size("expert")
    tokens_dev = grad_out.shape[0]
    width = grad_out.shape[1]
    hidden_width = hidden_saved.shape[2]
    examples_dev = clip_bound.shape[0]
    count_pairs = tokens_dev * TOPK
    capacity = min(tokens_dev, 2 * tokens_dev * TOPK // experts)
    ids_flat = expert_ids.reshape(count_pairs)
    onehot = (ids_flat[:, None] == jnp.arange(experts, dtype=jnp.int32)[None, :]).astype(jnp.int32)
    slot_ids = jnp.sum(jnp.cumsum(onehot, axis=0) * onehot, axis=1) - 1
    target = ids_flat * capacity + slot_ids
    hid_rows = hidden_saved.reshape(count_pairs, hidden_width)
    h_buffer = jnp.zeros((experts * capacity, hidden_width), jnp.bfloat16).at[target].set(hid_rows)
    h_buffer = h_buffer.reshape(experts, capacity, hidden_width)
    dy_pairs = jnp.repeat(grad_out, TOPK, axis=0)
    dy_buffer = jnp.zeros((experts * capacity, width), jnp.bfloat16).at[target].set(dy_pairs)
    dy_buffer = dy_buffer.reshape(experts, capacity, width)
    pair_info = jnp.stack(
        [
            gate_codes.reshape(count_pairs),
            jnp.arange(count_pairs, dtype=jnp.int32) // (EXLEN * TOPK),
        ],
        axis=1,
    ).astype(jnp.bfloat16)
    info_buffer = jnp.zeros((experts * capacity, 2), jnp.bfloat16).at[target].set(pair_info)
    info_buffer = info_buffer.reshape(experts, capacity, 2)
    recv_hidden, recv_dy, recv_info = (
        lax.all_to_all(h_buffer, "expert", split_axis=0, concat_axis=0, tiled=True),
        lax.all_to_all(dy_buffer, "expert", split_axis=0, concat_axis=0, tiled=True),
        lax.all_to_all(info_buffer, "expert", split_axis=0, concat_axis=0, tiled=True),
    )
    gate_recv = recv_info[:, :, 0].astype(jnp.float32) / 1024.0
    example_recv = recv_info[:, :, 1].astype(jnp.float32)
    owner_mask = (
        example_recv[:, :, None] == jnp.arange(examples_dev, dtype=jnp.float32)[None, None, :]
    ).astype(jnp.float32)
    hid_gram = jnp.einsum(
        "smh,snh->smn", recv_hidden, recv_hidden, preferred_element_type=jnp.float32
    )
    grad_gram = jnp.einsum("smd,snd->smn", recv_dy, recv_dy, preferred_element_type=jnp.float32)
    weights = hid_gram * grad_gram * gate_recv[:, :, None] * gate_recv[:, None, :]
    partial_value = jnp.sum(jnp.einsum("smn,snx->smx", weights, owner_mask) * owner_mask, axis=1)
    bounds_all = lax.all_gather(clip_bound, "expert", axis=0, tiled=True).reshape(
        experts, examples_dev
    )
    totals = lax.psum(partial_value, "expert")
    factor_all = jnp.minimum(1.0, bounds_all / jnp.sqrt(totals + 1e-06))
    factors = lax.dynamic_index_in_dim(factor_all, lax.axis_index("expert"), 0, keepdims=False)
    pair_scale = jnp.sum(owner_mask * factor_all[:, None, :], axis=2) * gate_recv
    recv_scaled = (pair_scale[:, :, None] * recv_dy.astype(jnp.float32)).astype(jnp.bfloat16)
    summed = lax.psum_scatter(
        lax.dot_general(
            recv_scaled,
            recv_hidden,
            (((0, 1), (0, 1)), ((), ())),
            preferred_element_type=jnp.float32,
        ).astype(jnp.bfloat16),
        "dp",
        scatter_dimension=0,
        tiled=True,
    )
    return (summed[None], factors)


def norm_kernel(experts, dy_ref, hid_ref, ids_ref, gate_ref, bound_ref, meta_ref, factor_ref):
    examples = bound_ref.shape[1]
    tokens = dy_ref.shape[0]
    pairs = EXLEN * TOPK
    spread = (
        lax.broadcasted_iota(jnp.int32, (pairs, EXLEN), 0) // TOPK
        == lax.broadcasted_iota(jnp.int32, (pairs, EXLEN), 1)
    ).astype(jnp.float32)
    token = lax.broadcasted_iota(jnp.int32, (tokens, tokens * TOPK), 0)
    place = lax.broadcasted_iota(jnp.int32, (tokens, tokens * TOPK), 1)
    widen = (token == place // TOPK).astype(jnp.float32).astype(jnp.bfloat16)
    codes = jnp.concatenate([ids_ref[...], gate_ref[...]], axis=0).astype(jnp.float32).astype(jnp.bfloat16)
    wide = jnp.dot(codes, widen, preferred_element_type=jnp.float32)
    rank = lax.broadcasted_iota(jnp.int32, wide.shape, 0)
    own = rank % TOPK == lax.broadcasted_iota(jnp.int32, wide.shape, 1) % TOPK
    wide = jnp.where(own, wide, 0.0)
    ids_all = jnp.sum(wide[:TOPK], axis=0, keepdims=True)
    gate_all = jnp.sum(wide[TOPK:], axis=0, keepdims=True) / 1024.0
    factor_row = jnp.zeros((1, examples), jnp.float32)
    for x in range(examples):
        ids_row = ids_all[:, x * pairs : (x + 1) * pairs]
        gate_row = gate_all[:, x * pairs : (x + 1) * pairs]
        hid = hid_ref[x * pairs : (x + 1) * pairs, :]
        dy = dy_ref[x * EXLEN : (x + 1) * EXLEN, :]
        hid_gram = lax.dot_general(hid, hid, (((1,), (1,)), ((), ())), preferred_element_type=jnp.float32)
        dy_gram = lax.dot_general(dy, dy, (((1,), (1,)), ((), ())), preferred_element_type=jnp.float32)
        half = jnp.dot(spread, dy_gram, precision=HIGHEST, preferred_element_type=jnp.float32)
        pair_gram = lax.dot_general(
            half, spread, (((1,), (1,)), ((), ())), precision=HIGHEST, preferred_element_type=jnp.float32
        )
        name = lax.broadcasted_iota(jnp.int32, (experts, pairs), 0).astype(jnp.float32)
        onehot = (name == ids_row).astype(jnp.float32)
        same = lax.dot_general(onehot, onehot, (((0,), (0,)), ((), ())), preferred_element_type=jnp.float32)
        weights = hid_gram * pair_gram * same
        sums = jnp.dot(gate_row, weights, precision=HIGHEST, preferred_element_type=jnp.float32)
        norm = jnp.sum(sums * gate_row, axis=1, keepdims=True)
        factor = jnp.minimum(1.0, bound_ref[:, x : x + 1] / jnp.sqrt(norm + 1e-06))
        lane = lax.broadcasted_iota(jnp.int32, (1, examples), 1)
        factor_row = jnp.where(lane == x, factor, factor_row)
        meta_ref[x : x + 1, :] = factor * gate_row
        meta_ref[examples + x : examples + x + 1, :] = ids_row
    factor_ref[...] = factor_row


def build_kernel(chips, place_ref, own_ref, sib_ref, own_meta_ref, sib_meta_ref, *out_refs):
    examples = own_meta_ref.shape[0] // 2
    pairs = EXLEN * TOPK
    rows = chips * EXLEN
    me = place_ref[0]
    row = lax.broadcasted_iota(jnp.int32, (rows, pairs), 0)
    lane = lax.broadcasted_iota(jnp.int32, (rows, pairs), 1)
    same_token = (row % EXLEN) == (lane // TOPK)
    expert = (lax.bitwise_xor(row // EXLEN, me // 2) * 2 + me % 2).astype(jnp.float32)
    for side, (hid_ref, meta_ref) in enumerate(((own_ref, own_meta_ref), (sib_ref, sib_meta_ref))):
        for x in range(examples):
            hit = same_token & (meta_ref[examples + x : examples + x + 1, :] == expert)
            scale = jnp.sum(jnp.where(hit, meta_ref[x : x + 1, :], 0.0), axis=1, keepdims=True)
            picked = jnp.dot(
                hit.astype(jnp.float32).astype(jnp.bfloat16),
                hid_ref[x * pairs : (x + 1) * pairs, :],
                preferred_element_type=jnp.float32,
            )
            message = (picked * scale).astype(jnp.bfloat16)
            start = (side * examples + x) * EXLEN
            for j in range(chips):
                out_refs[j][start : start + EXLEN, :] = message[j * EXLEN : (j + 1) * EXLEN, :]


def product_kernel(places, count, has_total, *refs):
    dy_refs, hid_refs, out_ref = refs[:count], refs[count : count + len(places)], refs[-1]
    total = refs[-2][...] if has_total else None
    for hid_ref, sides in zip(hid_refs, places):
        dy = jnp.concatenate([dy_refs[k][begin : begin + rows, :] for k, begin, rows in sides], axis=0)
        term = lax.dot_general(
            dy, hid_ref[...], (((0,), (0,)), ((), ())), preferred_element_type=jnp.float32
        )
        total = term if total is None else total + term
    out_ref[...] = total.astype(out_ref.dtype)


def product(name, offsets, slots, where, total, dtype):
    arrays, places = [], []
    for j in offsets:
        sides = []
        for array, begin, rows in where[j]:
            known = [k for k, other in enumerate(arrays) if other is array]
            if not known:
                arrays.append(array)
            sides.append((known[0] if known else len(arrays) - 1, begin, rows))
        places.append(sides)
    width, hidden = arrays[0].shape[1], slots[0].shape[1]
    block = min(width, 256)
    operands = arrays + [slots[j] for j in offsets]
    specs = [pl.BlockSpec((array.shape[0], block), lambda i: (0, i)) for array in arrays]
    specs += [pl.BlockSpec(slots[j].shape, lambda i: (0, 0)) for j in offsets]
    if total is not None:
        operands.append(total)
        specs.append(pl.BlockSpec((block, hidden), lambda i: (i, 0)))
    return pl.pallas_call(
        functools.partial(product_kernel, places, len(arrays), total is not None),
        out_shape=jax.ShapeDtypeStruct((width, hidden), dtype),
        grid=(width // block,),
        in_specs=specs,
        out_specs=pl.BlockSpec((block, hidden), lambda i: (i, 0)),
        compiler_params=pltpu.CompilerParams(vmem_limit_bytes=VMEM_LIMIT),
        cost_estimate=pl.CostEstimate(
            flops=2 * width * hidden * sum(slots[j].shape[0] for j in offsets),
            bytes_accessed=sum(a.size * a.dtype.itemsize for a in operands) + width * hidden * 4,
            transcendentals=0,
        ),
        name=name,
    )(*operands)


def per_device_dense(hidden_saved, grad_out, expert_ids, gate_codes, clip_bound):
    devices = lax.axis_size("expert")
    chips = devices // 2
    tokens, width = grad_out.shape
    hidden = hidden_saved.shape[2]
    examples = clip_bound.shape[0]
    pairs = EXLEN * TOPK
    me = lax.axis_index("expert")
    params = pltpu.CompilerParams(vmem_limit_bytes=VMEM_LIMIT)

    def swap(array, offset):
        return lax.ppermute(array, "expert", [(i, i ^ offset) for i in range(devices)])

    def after(arrays, done):
        return lax.optimization_barrier(tuple(arrays) + tuple(done))[: len(arrays)]

    hid_rows = hidden_saved.reshape(tokens * TOPK, hidden)
    sib_rows = swap(hid_rows, 1)
    dy_z2, dy_z1, dy_x = swap(grad_out, 8), swap(grad_out, 4), swap(grad_out, 2)
    meta, factors = pl.pallas_call(
        functools.partial(norm_kernel, devices),
        out_shape=(
            jax.ShapeDtypeStruct((2 * examples, pairs), jnp.float32),
            jax.ShapeDtypeStruct((1, examples), jnp.float32),
        ),
        compiler_params=params,
        name="norms",
    )(grad_out, hid_rows, expert_ids.T, gate_codes.T, clip_bound.reshape(1, examples))
    sib_meta = swap(meta, 1)
    slots = pl.pallas_call(
        functools.partial(build_kernel, chips),
        out_shape=[jax.ShapeDtypeStruct((2 * tokens, hidden), jnp.bfloat16)] * chips,
        in_specs=[pl.BlockSpec(memory_space=pltpu.SMEM)] + [pl.BlockSpec(memory_space=pltpu.VMEM)] * 4,
        compiler_params=params,
        name="build",
    )(me.astype(jnp.int32).reshape(1), hid_rows, sib_rows, meta, sib_meta)
    slots = list(slots)
    slots[1] = swap(slots[1], 2)
    first = (dy_z2, dy_z1, dy_x, slots[1])

    near = jnp.concatenate([grad_out, dy_z1, dy_x, dy_z2])
    both = jnp.concatenate([dy_z1, dy_z2])
    slot4, slot6, slot3, dy_z2b, both, near = after((slots[4], slots[6], slots[3], dy_z2, both, near), first)
    slots[4], slots[6], slots[3] = swap(slot4, 8), swap(slot6, 12), swap(slot3, 6)
    dy_z3, dy_xz, sib_near = swap(dy_z2b, 4), swap(both, 2), swap(near, 1)
    second = (slots[4], slots[6], slots[3], dy_z3, dy_xz, sib_near)

    far = jnp.concatenate([dy_z3, dy_xz])
    slot5, slot7, slot2, dy_z3b, far = after((slots[5], slots[7], slots[2], dy_z3, far), second)
    slots[5], slots[7], slots[2] = swap(slot5, 10), swap(slot7, 14), swap(slot2, 4)
    dy_xz3, sib_far = swap(dy_z3b, 2), swap(far, 1)
    third = (slots[5], slots[7], slots[2], dy_xz3, sib_far)
    sib_last = swap(after((dy_xz3,), third)[0], 1)

    t = tokens
    where = {
        0: [(grad_out, 0, t), (sib_near, 0, t)],
        1: [(dy_x, 0, t), (sib_near, 2 * t, t)],
        2: [(dy_z1, 0, t), (sib_near, t, t)],
        3: [(dy_xz, 0, t), (sib_far, t, t)],
        4: [(dy_z2, 0, t), (sib_near, 3 * t, t)],
        5: [(dy_xz, t, t), (sib_far, 2 * t, t)],
        6: [(dy_z3, 0, t), (sib_far, 0, t)],
        7: [(dy_xz3, 0, t), (sib_last, 0, t)],
    }
    summed = product("product", range(chips), slots, where, None, jnp.bfloat16)
    return (summed[None], factors.reshape(examples))


def solution(mesh):
    def per_device(hidden_saved, grad_out, expert_ids, gate_codes, clip_bound):
        devices = mesh.shape["expert"]
        tokens = grad_out.shape[0]
        dense = (
            mesh.shape["dp"] == 1
            and devices == 16
            and 2 * tokens * TOPK // devices >= tokens
        )
        run = per_device_dense if dense else per_device_sparse
        return run(hidden_saved, grad_out, expert_ids, gate_codes, clip_bound)

    return jax.shard_map(
        per_device,
        mesh=mesh,
        in_specs=(
            P(("groups", "expert", "dp"), None, None),
            P(("groups", "expert", "dp"), None),
            P(("groups", "expert", "dp"), None),
            P(("groups", "expert", "dp"), None),
            P(("groups", "expert", "dp")),
        ),
        out_specs=(P(("groups", "expert"), "dp", None), P(("groups", "expert", "dp"))),
        check_vma=False,
    )
```

```python
import functools

import jax
import jax.numpy as jnp
from jax import lax
from jax.experimental import pallas as pl
from jax.experimental.pallas import tpu as pltpu
from jax.sharding import PartitionSpec as P

TOPK = 8
EXLEN = 32
VMEM_LIMIT = 16 * 1024 * 1024
PRODUCT_LIMIT = 32 * 1024 * 1024
LATE_BLOCK = 1024
HIGHEST = lax.Precision.HIGHEST


def per_device_sparse(hidden_saved, grad_out, expert_ids, gate_codes, clip_bound):
    experts = lax.axis_size("expert")
    tokens_dev = grad_out.shape[0]
    width = grad_out.shape[1]
    hidden_width = hidden_saved.shape[2]
    examples_dev = clip_bound.shape[0]
    count_pairs = tokens_dev * TOPK
    capacity = min(tokens_dev, 2 * tokens_dev * TOPK // experts)
    ids_flat = expert_ids.reshape(count_pairs)
    onehot = (ids_flat[:, None] == jnp.arange(experts, dtype=jnp.int32)[None, :]).astype(jnp.int32)
    slot_ids = jnp.sum(jnp.cumsum(onehot, axis=0) * onehot, axis=1) - 1
    target = ids_flat * capacity + slot_ids
    hid_rows = hidden_saved.reshape(count_pairs, hidden_width)
    h_buffer = jnp.zeros((experts * capacity, hidden_width), jnp.bfloat16).at[target].set(hid_rows)
    h_buffer = h_buffer.reshape(experts, capacity, hidden_width)
    dy_pairs = jnp.repeat(grad_out, TOPK, axis=0)
    dy_buffer = jnp.zeros((experts * capacity, width), jnp.bfloat16).at[target].set(dy_pairs)
    dy_buffer = dy_buffer.reshape(experts, capacity, width)
    pair_info = jnp.stack(
        [
            gate_codes.reshape(count_pairs),
            jnp.arange(count_pairs, dtype=jnp.int32) // (EXLEN * TOPK),
        ],
        axis=1,
    ).astype(jnp.bfloat16)
    info_buffer = jnp.zeros((experts * capacity, 2), jnp.bfloat16).at[target].set(pair_info)
    info_buffer = info_buffer.reshape(experts, capacity, 2)
    recv_hidden, recv_dy, recv_info = (
        lax.all_to_all(h_buffer, "expert", split_axis=0, concat_axis=0, tiled=True),
        lax.all_to_all(dy_buffer, "expert", split_axis=0, concat_axis=0, tiled=True),
        lax.all_to_all(info_buffer, "expert", split_axis=0, concat_axis=0, tiled=True),
    )
    gate_recv = recv_info[:, :, 0].astype(jnp.float32) / 1024.0
    example_recv = recv_info[:, :, 1].astype(jnp.float32)
    owner_mask = (
        example_recv[:, :, None] == jnp.arange(examples_dev, dtype=jnp.float32)[None, None, :]
    ).astype(jnp.float32)
    hid_gram = jnp.einsum(
        "smh,snh->smn", recv_hidden, recv_hidden, preferred_element_type=jnp.float32
    )
    grad_gram = jnp.einsum("smd,snd->smn", recv_dy, recv_dy, preferred_element_type=jnp.float32)
    weights = hid_gram * grad_gram * gate_recv[:, :, None] * gate_recv[:, None, :]
    partial_value = jnp.sum(jnp.einsum("smn,snx->smx", weights, owner_mask) * owner_mask, axis=1)
    bounds_all = lax.all_gather(clip_bound, "expert", axis=0, tiled=True).reshape(
        experts, examples_dev
    )
    totals = lax.psum(partial_value, "expert")
    factor_all = jnp.minimum(1.0, bounds_all / jnp.sqrt(totals + 1e-06))
    factors = lax.dynamic_index_in_dim(factor_all, lax.axis_index("expert"), 0, keepdims=False)
    pair_scale = jnp.sum(owner_mask * factor_all[:, None, :], axis=2) * gate_recv
    recv_scaled = (pair_scale[:, :, None] * recv_dy.astype(jnp.float32)).astype(jnp.bfloat16)
    summed = lax.psum_scatter(
        lax.dot_general(
            recv_scaled,
            recv_hidden,
            (((0, 1), (0, 1)), ((), ())),
            preferred_element_type=jnp.float32,
        ).astype(jnp.bfloat16),
        "dp",
        scatter_dimension=0,
        tiled=True,
    )
    return (summed[None], factors)


def norm_kernel(experts, dy_ref, hid_ref, ids_ref, gate_ref, bound_ref, meta_ref, factor_ref):
    examples = bound_ref.shape[1]
    tokens = dy_ref.shape[0]
    pairs = EXLEN * TOPK
    spread = (
        lax.broadcasted_iota(jnp.int32, (pairs, EXLEN), 0) // TOPK
        == lax.broadcasted_iota(jnp.int32, (pairs, EXLEN), 1)
    ).astype(jnp.float32)
    token = lax.broadcasted_iota(jnp.int32, (tokens, tokens * TOPK), 0)
    place = lax.broadcasted_iota(jnp.int32, (tokens, tokens * TOPK), 1)
    widen = (token == place // TOPK).astype(jnp.float32).astype(jnp.bfloat16)
    codes = jnp.concatenate([ids_ref[...], gate_ref[...]], axis=0).astype(jnp.float32).astype(jnp.bfloat16)
    wide = jnp.dot(codes, widen, preferred_element_type=jnp.float32)
    rank = lax.broadcasted_iota(jnp.int32, wide.shape, 0)
    own = rank % TOPK == lax.broadcasted_iota(jnp.int32, wide.shape, 1) % TOPK
    wide = jnp.where(own, wide, 0.0)
    ids_all = jnp.sum(wide[:TOPK], axis=0, keepdims=True)
    gate_all = jnp.sum(wide[TOPK:], axis=0, keepdims=True) / 1024.0
    factor_row = jnp.zeros((1, examples), jnp.float32)
    for x in range(examples):
        ids_row = ids_all[:, x * pairs : (x + 1) * pairs]
        gate_row = gate_all[:, x * pairs : (x + 1) * pairs]
        hid = hid_ref[x * pairs : (x + 1) * pairs, :]
        dy = dy_ref[x * EXLEN : (x + 1) * EXLEN, :]
        hid_gram = lax.dot_general(hid, hid, (((1,), (1,)), ((), ())), preferred_element_type=jnp.float32)
        dy_gram = lax.dot_general(dy, dy, (((1,), (1,)), ((), ())), preferred_element_type=jnp.float32)
        half = jnp.dot(spread, dy_gram, precision=HIGHEST, preferred_element_type=jnp.float32)
        pair_gram = lax.dot_general(
            half, spread, (((1,), (1,)), ((), ())), precision=HIGHEST, preferred_element_type=jnp.float32
        )
        name = lax.broadcasted_iota(jnp.int32, (experts, pairs), 0).astype(jnp.float32)
        onehot = (name == ids_row).astype(jnp.float32)
        same = lax.dot_general(onehot, onehot, (((0,), (0,)), ((), ())), preferred_element_type=jnp.float32)
        weights = hid_gram * pair_gram * same
        sums = jnp.dot(gate_row, weights, precision=HIGHEST, preferred_element_type=jnp.float32)
        norm = jnp.sum(sums * gate_row, axis=1, keepdims=True)
        factor = jnp.minimum(1.0, bound_ref[:, x : x + 1] / jnp.sqrt(norm + 1e-06))
        lane = lax.broadcasted_iota(jnp.int32, (1, examples), 1)
        factor_row = jnp.where(lane == x, factor, factor_row)
        meta_ref[x : x + 1, :] = factor * gate_row
        meta_ref[examples + x : examples + x + 1, :] = ids_row
    factor_ref[...] = factor_row


def build_kernel(chips, place_ref, own_ref, sib_ref, own_meta_ref, sib_meta_ref, *out_refs):
    examples = own_meta_ref.shape[0] // 2
    pairs = EXLEN * TOPK
    rows = chips * EXLEN
    me = place_ref[0]
    row = lax.broadcasted_iota(jnp.int32, (rows, pairs), 0)
    lane = lax.broadcasted_iota(jnp.int32, (rows, pairs), 1)
    same_token = (row % EXLEN) == (lane // TOPK)
    expert = (lax.bitwise_xor(row // EXLEN, me // 2) * 2 + me % 2).astype(jnp.float32)
    for side, (hid_ref, meta_ref) in enumerate(((own_ref, own_meta_ref), (sib_ref, sib_meta_ref))):
        for x in range(examples):
            hit = same_token & (meta_ref[examples + x : examples + x + 1, :] == expert)
            scale = jnp.sum(jnp.where(hit, meta_ref[x : x + 1, :], 0.0), axis=1, keepdims=True)
            picked = jnp.dot(
                hit.astype(jnp.float32).astype(jnp.bfloat16),
                hid_ref[x * pairs : (x + 1) * pairs, :],
                preferred_element_type=jnp.float32,
            )
            message = (picked * scale).astype(jnp.bfloat16)
            start = (side * examples + x) * EXLEN
            for j in range(chips):
                out_refs[j][start : start + EXLEN, :] = message[j * EXLEN : (j + 1) * EXLEN, :]


def product_kernel(places, block, has_total, *refs):
    m = len(places)
    n = len(refs) - m - 3 - has_total
    dy_refs, hid_refs, (out_ref, out_tiles, out_sems) = refs[:n], refs[n : n + m], refs[n + m + has_total :]
    chunks = out_ref.shape[0] // block

    def out_copy(c):
        return pltpu.make_async_copy(
            out_tiles.at[c % 2], out_ref.at[pl.ds(c * block, block), :], out_sems.at[c % 2]
        )

    for c in range(chunks):
        if c >= 2:
            out_copy(c - 2).wait()
        columns = slice(c * block, (c + 1) * block)
        dy = jnp.concatenate(
            [dy_refs[k][begin : begin + rows, columns] for sides in places for k, begin, rows in sides], axis=0
        )
        hid = jnp.concatenate([hid_ref[...] for hid_ref in hid_refs], axis=0)
        value = lax.dot_general(dy, hid, (((0,), (0,)), ((), ())), preferred_element_type=jnp.float32)
        if has_total:
            value = value + refs[n + m][columns, :]
        out_tiles[c % 2] = value.astype(out_tiles.dtype)
        out_copy(c).start()
    for c in range(max(chunks - 2, 0), chunks):
        out_copy(c).wait()


def early_kernel(places, block, *refs):
    m = len(places)
    n = len(refs) - m - 1
    dy_refs, hid_refs, out_ref = refs[:n], refs[n : n + m], refs[n + m]
    for c in range(out_ref.shape[0] // block):
        columns = slice(c * block, (c + 1) * block)
        dy = jnp.concatenate(
            [dy_refs[k][begin : begin + rows, columns] for sides in places for k, begin, rows in sides], axis=0
        )
        hid = jnp.concatenate([hid_ref[...] for hid_ref in hid_refs], axis=0)
        out_ref[columns, :] = lax.dot_general(dy, hid, (((0,), (0,)), ((), ())), preferred_element_type=jnp.float32)


def product(offsets, slots, where, early, total=None):
    arrays, places = [], []
    for j in offsets:
        sides = []
        for array, begin, rows in where[j]:
            known = [k for k, other in enumerate(arrays) if other is array]
            if not known:
                arrays.append(array)
            sides.append((known[0] if known else len(arrays) - 1, begin, rows))
        places.append(sides)
    width, hidden = arrays[0].shape[1], slots[0].shape[1]
    operands = arrays + [slots[j] for j in offsets] + ([] if total is None else [total])
    if early:
        block = min(width, 512)
        kernel = functools.partial(early_kernel, places, block)
        out_space, scratch = pltpu.VMEM, ()
    else:
        block = min(width, LATE_BLOCK)
        kernel = functools.partial(product_kernel, places, block, int(total is not None))
        out_space = pl.ANY
        scratch = (pltpu.VMEM((2, block, hidden), jnp.bfloat16), pltpu.SemaphoreType.DMA((2,)))
    return pl.pallas_call(
        kernel,
        out_shape=jax.ShapeDtypeStruct((width, hidden), jnp.float32 if early else jnp.bfloat16),
        in_specs=[pl.BlockSpec(memory_space=pltpu.VMEM)] * len(operands),
        out_specs=pl.BlockSpec(memory_space=out_space),
        scratch_shapes=scratch,
        compiler_params=pltpu.CompilerParams(vmem_limit_bytes=PRODUCT_LIMIT),
        cost_estimate=pl.CostEstimate(
            flops=2 * width * hidden * sum(slots[j].shape[0] for j in offsets),
            bytes_accessed=2 * width * hidden,
            transcendentals=0,
        ),
        name="early_product" if early else "product",
    )(*operands)


def per_device_dense(hidden_saved, grad_out, expert_ids, gate_codes, clip_bound):
    devices = lax.axis_size("expert")
    chips = devices // 2
    tokens, width = grad_out.shape
    hidden = hidden_saved.shape[2]
    examples = clip_bound.shape[0]
    pairs = EXLEN * TOPK
    me = lax.axis_index("expert")
    params = pltpu.CompilerParams(vmem_limit_bytes=VMEM_LIMIT)

    def swap(array, offset):
        return lax.ppermute(array, "expert", [(i, i ^ offset) for i in range(devices)])

    def after(arrays, done):
        return lax.optimization_barrier(tuple(arrays) + tuple(done))[: len(arrays)]

    hid_rows = hidden_saved.reshape(tokens * TOPK, hidden)
    sib_rows = swap(hid_rows, 1)
    dy_z2, dy_z1, dy_x = swap(grad_out, 8), swap(grad_out, 4), swap(grad_out, 2)
    meta, factors = pl.pallas_call(
        functools.partial(norm_kernel, devices),
        out_shape=(
            jax.ShapeDtypeStruct((2 * examples, pairs), jnp.float32),
            jax.ShapeDtypeStruct((1, examples), jnp.float32),
        ),
        compiler_params=params,
        name="norms",
    )(grad_out, hid_rows, expert_ids.T, gate_codes.T, clip_bound.reshape(1, examples))
    sib_meta = swap(meta, 1)
    slots = pl.pallas_call(
        functools.partial(build_kernel, chips),
        out_shape=[jax.ShapeDtypeStruct((2 * tokens, hidden), jnp.bfloat16)] * chips,
        in_specs=[pl.BlockSpec(memory_space=pltpu.SMEM)] + [pl.BlockSpec(memory_space=pltpu.VMEM)] * 4,
        compiler_params=params,
        name="build",
    )(me.astype(jnp.int32).reshape(1), hid_rows, sib_rows, meta, sib_meta)
    slots = list(slots)
    slots[1] = swap(slots[1], 2)
    first = (dy_z2, dy_z1, dy_x, slots[1])

    near = jnp.concatenate([grad_out, dy_z1, dy_x, dy_z2])
    both = jnp.concatenate([dy_z1, dy_z2])
    slot4, slot6, slot3, dy_z2b, both, near = after((slots[4], slots[6], slots[3], dy_z2, both, near), first)
    slots[4], slots[6], slots[3] = swap(slot4, 8), swap(slot6, 12), swap(slot3, 6)
    dy_z3, dy_xz, sib_near = swap(dy_z2b, 4), swap(both, 2), swap(near, 1)
    second = (slots[4], slots[6], slots[3], dy_z3, dy_xz, sib_near)

    far = jnp.concatenate([dy_z3, dy_xz])
    t = tokens
    slot5, slot7, slot2, dy_z3b, far = after((slots[5], slots[7], slots[2], dy_z3, far), second)
    dy_xz3, sib_far = swap(dy_z3b, 2), swap(far, 1)
    where = {
        0: [(grad_out, 0, t), (sib_near, 0, t)],
        1: [(dy_x, 0, t), (sib_near, 2 * t, t)],
        2: [(dy_z1, 0, t), (sib_near, t, t)],
        3: [(dy_xz, 0, t), (sib_far, t, t)],
        4: [(dy_z2, 0, t), (sib_near, 3 * t, t)],
        5: [(dy_xz, t, t), (sib_far, 2 * t, t)],
        6: [(dy_z3, 0, t), (sib_far, 0, t)],
    }
    slots[5], slots[7], slots[2] = swap(slot5, 10), swap(slot7, 14), swap(slot2, 4)
    third = (slots[5], slots[7], slots[2], dy_xz3, sib_far)
    total = product((0, 1, 4, 3, 6), slots, where, True)
    sib_last = swap(after((dy_xz3,), third + (total,))[0], 1)
    where[7] = [(dy_xz3, 0, t), (sib_last, 0, t)]
    rest = [j for j in (3, 6, 5, 2, 7) if j not in (0, 1, 4, 3, 6)]
    summed = product(rest, slots, where, False, total)
    return (summed[None], factors.reshape(examples))


def solution(mesh):
    def per_device(hidden_saved, grad_out, expert_ids, gate_codes, clip_bound):
        devices = mesh.shape["expert"]
        tokens = grad_out.shape[0]
        dense = (
            mesh.shape["dp"] == 1
            and devices == 16
            and 2 * tokens * TOPK // devices >= tokens
        )
        run = per_device_dense if dense else per_device_sparse
        return run(hidden_saved, grad_out, expert_ids, gate_codes, clip_bound)

    return jax.shard_map(
        per_device,
        mesh=mesh,
        in_specs=(
            P(("groups", "expert", "dp"), None, None),
            P(("groups", "expert", "dp"), None),
            P(("groups", "expert", "dp"), None),
            P(("groups", "expert", "dp"), None),
            P(("groups", "expert", "dp")),
        ),
        out_specs=(P(("groups", "expert"), "dp", None), P(("groups", "expert", "dp"))),
        check_vma=False,
    )
```

```python
import functools

import jax
import jax.numpy as jnp
from jax import lax
from jax.experimental import pallas as pl
from jax.experimental.pallas import tpu as pltpu
from jax.sharding import PartitionSpec as P

TOPK = 8
EXLEN = 32
VMEM_LIMIT = 16 * 1024 * 1024
PRODUCT_LIMIT = 32 * 1024 * 1024
LATE_BLOCK = 1024
HIGHEST = lax.Precision.HIGHEST


def per_device_sparse(hidden_saved, grad_out, expert_ids, gate_codes, clip_bound):
    experts = lax.axis_size("expert")
    tokens_dev = grad_out.shape[0]
    width = grad_out.shape[1]
    hidden_width = hidden_saved.shape[2]
    examples_dev = clip_bound.shape[0]
    count_pairs = tokens_dev * TOPK
    capacity = min(tokens_dev, 2 * tokens_dev * TOPK // experts)
    ids_flat = expert_ids.reshape(count_pairs)
    onehot = (ids_flat[:, None] == jnp.arange(experts, dtype=jnp.int32)[None, :]).astype(jnp.int32)
    slot_ids = jnp.sum(jnp.cumsum(onehot, axis=0) * onehot, axis=1) - 1
    target = ids_flat * capacity + slot_ids
    hid_rows = hidden_saved.reshape(count_pairs, hidden_width)
    h_buffer = jnp.zeros((experts * capacity, hidden_width), jnp.bfloat16).at[target].set(hid_rows)
    h_buffer = h_buffer.reshape(experts, capacity, hidden_width)
    dy_pairs = jnp.repeat(grad_out, TOPK, axis=0)
    dy_buffer = jnp.zeros((experts * capacity, width), jnp.bfloat16).at[target].set(dy_pairs)
    dy_buffer = dy_buffer.reshape(experts, capacity, width)
    pair_info = jnp.stack(
        [
            gate_codes.reshape(count_pairs),
            jnp.arange(count_pairs, dtype=jnp.int32) // (EXLEN * TOPK),
        ],
        axis=1,
    ).astype(jnp.bfloat16)
    info_buffer = jnp.zeros((experts * capacity, 2), jnp.bfloat16).at[target].set(pair_info)
    info_buffer = info_buffer.reshape(experts, capacity, 2)
    recv_hidden, recv_dy, recv_info = (
        lax.all_to_all(h_buffer, "expert", split_axis=0, concat_axis=0, tiled=True),
        lax.all_to_all(dy_buffer, "expert", split_axis=0, concat_axis=0, tiled=True),
        lax.all_to_all(info_buffer, "expert", split_axis=0, concat_axis=0, tiled=True),
    )
    gate_recv = recv_info[:, :, 0].astype(jnp.float32) / 1024.0
    example_recv = recv_info[:, :, 1].astype(jnp.float32)
    owner_mask = (
        example_recv[:, :, None] == jnp.arange(examples_dev, dtype=jnp.float32)[None, None, :]
    ).astype(jnp.float32)
    hid_gram = jnp.einsum(
        "smh,snh->smn", recv_hidden, recv_hidden, preferred_element_type=jnp.float32
    )
    grad_gram = jnp.einsum("smd,snd->smn", recv_dy, recv_dy, preferred_element_type=jnp.float32)
    weights = hid_gram * grad_gram * gate_recv[:, :, None] * gate_recv[:, None, :]
    partial_value = jnp.sum(jnp.einsum("smn,snx->smx", weights, owner_mask) * owner_mask, axis=1)
    bounds_all = lax.all_gather(clip_bound, "expert", axis=0, tiled=True).reshape(
        experts, examples_dev
    )
    totals = lax.psum(partial_value, "expert")
    factor_all = jnp.minimum(1.0, bounds_all / jnp.sqrt(totals + 1e-06))
    factors = lax.dynamic_index_in_dim(factor_all, lax.axis_index("expert"), 0, keepdims=False)
    pair_scale = jnp.sum(owner_mask * factor_all[:, None, :], axis=2) * gate_recv
    recv_scaled = (pair_scale[:, :, None] * recv_dy.astype(jnp.float32)).astype(jnp.bfloat16)
    summed = lax.psum_scatter(
        lax.dot_general(
            recv_scaled,
            recv_hidden,
            (((0, 1), (0, 1)), ((), ())),
            preferred_element_type=jnp.float32,
        ).astype(jnp.bfloat16),
        "dp",
        scatter_dimension=0,
        tiled=True,
    )
    return (summed[None], factors)


def norm_kernel(experts, dy_ref, hid_ref, ids_ref, gate_ref, bound_ref, meta_ref, factor_ref):
    examples = bound_ref.shape[1]
    tokens = dy_ref.shape[0]
    pairs = EXLEN * TOPK
    spread = (
        lax.broadcasted_iota(jnp.int32, (pairs, EXLEN), 0) // TOPK
        == lax.broadcasted_iota(jnp.int32, (pairs, EXLEN), 1)
    ).astype(jnp.float32)
    token = lax.broadcasted_iota(jnp.int32, (tokens, tokens * TOPK), 0)
    place = lax.broadcasted_iota(jnp.int32, (tokens, tokens * TOPK), 1)
    widen = (token == place // TOPK).astype(jnp.float32).astype(jnp.bfloat16)
    codes = jnp.concatenate([ids_ref[...], gate_ref[...]], axis=0).astype(jnp.float32).astype(jnp.bfloat16)
    wide = jnp.dot(codes, widen, preferred_element_type=jnp.float32)
    rank = lax.broadcasted_iota(jnp.int32, wide.shape, 0)
    own = rank % TOPK == lax.broadcasted_iota(jnp.int32, wide.shape, 1) % TOPK
    wide = jnp.where(own, wide, 0.0)
    ids_all = jnp.sum(wide[:TOPK], axis=0, keepdims=True)
    gate_all = jnp.sum(wide[TOPK:], axis=0, keepdims=True) / 1024.0
    factor_row = jnp.zeros((1, examples), jnp.float32)
    for x in range(examples):
        ids_row = ids_all[:, x * pairs : (x + 1) * pairs]
        gate_row = gate_all[:, x * pairs : (x + 1) * pairs]
        hid = hid_ref[x * pairs : (x + 1) * pairs, :]
        dy = dy_ref[x * EXLEN : (x + 1) * EXLEN, :]
        hid_gram = lax.dot_general(hid, hid, (((1,), (1,)), ((), ())), preferred_element_type=jnp.float32)
        dy_gram = lax.dot_general(dy, dy, (((1,), (1,)), ((), ())), preferred_element_type=jnp.float32)
        half = jnp.dot(spread, dy_gram, precision=HIGHEST, preferred_element_type=jnp.float32)
        pair_gram = lax.dot_general(
            half, spread, (((1,), (1,)), ((), ())), precision=HIGHEST, preferred_element_type=jnp.float32
        )
        name = lax.broadcasted_iota(jnp.int32, (experts, pairs), 0).astype(jnp.float32)
        onehot = (name == ids_row).astype(jnp.float32)
        same = lax.dot_general(onehot, onehot, (((0,), (0,)), ((), ())), preferred_element_type=jnp.float32)
        weights = hid_gram * pair_gram * same
        sums = jnp.dot(gate_row, weights, precision=HIGHEST, preferred_element_type=jnp.float32)
        norm = jnp.sum(sums * gate_row, axis=1, keepdims=True)
        factor = jnp.minimum(1.0, bound_ref[:, x : x + 1] / jnp.sqrt(norm + 1e-06))
        lane = lax.broadcasted_iota(jnp.int32, (1, examples), 1)
        factor_row = jnp.where(lane == x, factor, factor_row)
        meta_ref[x : x + 1, :] = factor * gate_row
        meta_ref[examples + x : examples + x + 1, :] = ids_row
    factor_ref[...] = factor_row


def build_kernel(chips, place_ref, own_ref, sib_ref, own_meta_ref, sib_meta_ref, *out_refs):
    examples = own_meta_ref.shape[0] // 2
    pairs = EXLEN * TOPK
    rows = chips * EXLEN
    me = place_ref[0]
    row = lax.broadcasted_iota(jnp.int32, (rows, pairs), 0)
    lane = lax.broadcasted_iota(jnp.int32, (rows, pairs), 1)
    same_token = (row % EXLEN) == (lane // TOPK)
    expert = (lax.bitwise_xor(row // EXLEN, me // 2) * 2 + me % 2).astype(jnp.float32)
    for side, (hid_ref, meta_ref) in enumerate(((own_ref, own_meta_ref), (sib_ref, sib_meta_ref))):
        for x in range(examples):
            hit = same_token & (meta_ref[examples + x : examples + x + 1, :] == expert)
            scale = jnp.sum(jnp.where(hit, meta_ref[x : x + 1, :], 0.0), axis=1, keepdims=True)
            picked = jnp.dot(
                hit.astype(jnp.float32).astype(jnp.bfloat16),
                hid_ref[x * pairs : (x + 1) * pairs, :],
                preferred_element_type=jnp.float32,
            )
            message = (picked * scale).astype(jnp.bfloat16)
            start = (side * examples + x) * EXLEN
            for j in range(chips):
                out_refs[j][start : start + EXLEN, :] = message[j * EXLEN : (j + 1) * EXLEN, :]


def product_kernel(places, block, has_total, *refs):
    m = len(places)
    n = len(refs) - m - 3 - has_total
    dy_refs, hid_refs, (out_ref, out_tiles, out_sems) = refs[:n], refs[n : n + m], refs[n + m + has_total :]
    chunks = out_ref.shape[0] // block

    def out_copy(c):
        return pltpu.make_async_copy(
            out_tiles.at[c % 2], out_ref.at[pl.ds(c * block, block), :], out_sems.at[c % 2]
        )

    for c in range(chunks):
        if c >= 2:
            out_copy(c - 2).wait()
        columns = slice(c * block, (c + 1) * block)
        dy = jnp.concatenate(
            [dy_refs[k][begin : begin + rows, columns] for sides in places for k, begin, rows in sides], axis=0
        )
        hid = jnp.concatenate([hid_ref[...] for hid_ref in hid_refs], axis=0)
        value = lax.dot_general(dy, hid, (((0,), (0,)), ((), ())), preferred_element_type=jnp.float32)
        if has_total:
            value = value + refs[n + m][columns, :]
        out_tiles[c % 2] = value.astype(out_tiles.dtype)
        out_copy(c).start()
    for c in range(max(chunks - 2, 0), chunks):
        out_copy(c).wait()


def early_kernel(places, block, *refs):
    m = len(places)
    n = len(refs) - m - 1
    dy_refs, hid_refs, out_ref = refs[:n], refs[n : n + m], refs[n + m]
    for c in range(out_ref.shape[0] // block):
        columns = slice(c * block, (c + 1) * block)
        dy = jnp.concatenate(
            [dy_refs[k][begin : begin + rows, columns] for sides in places for k, begin, rows in sides], axis=0
        )
        hid = jnp.concatenate([hid_ref[...] for hid_ref in hid_refs], axis=0)
        out_ref[columns, :] = lax.dot_general(dy, hid, (((0,), (0,)), ((), ())), preferred_element_type=jnp.float32)


def product(offsets, slots, where, early, total=None):
    arrays, places = [], []
    for j in offsets:
        sides = []
        for array, begin, rows in where[j]:
            known = [k for k, other in enumerate(arrays) if other is array]
            if not known:
                arrays.append(array)
            sides.append((known[0] if known else len(arrays) - 1, begin, rows))
        places.append(sides)
    width, hidden = arrays[0].shape[1], slots[0].shape[1]
    operands = arrays + [slots[j] for j in offsets] + ([] if total is None else [total])
    if early:
        block = min(width, 512)
        kernel = functools.partial(early_kernel, places, block)
        out_space, scratch = pltpu.VMEM, ()
    else:
        block = min(width, LATE_BLOCK)
        kernel = functools.partial(product_kernel, places, block, int(total is not None))
        out_space = pl.ANY
        scratch = (pltpu.VMEM((2, block, hidden), jnp.bfloat16), pltpu.SemaphoreType.DMA((2,)))
    return pl.pallas_call(
        kernel,
        out_shape=jax.ShapeDtypeStruct((width, hidden), jnp.float32 if early else jnp.bfloat16),
        in_specs=[pl.BlockSpec(memory_space=pltpu.VMEM)] * len(operands),
        out_specs=pl.BlockSpec(memory_space=out_space),
        scratch_shapes=scratch,
        compiler_params=pltpu.CompilerParams(vmem_limit_bytes=PRODUCT_LIMIT),
        cost_estimate=pl.CostEstimate(
            flops=2 * width * hidden * sum(slots[j].shape[0] for j in offsets),
            bytes_accessed=2 * width * hidden,
            transcendentals=0,
        ),
        name="early_product" if early else "product",
    )(*operands)


def per_device_dense(hidden_saved, grad_out, expert_ids, gate_codes, clip_bound):
    devices = lax.axis_size("expert")
    chips = devices // 2
    tokens, width = grad_out.shape
    hidden = hidden_saved.shape[2]
    examples = clip_bound.shape[0]
    pairs = EXLEN * TOPK
    me = lax.axis_index("expert")
    params = pltpu.CompilerParams(vmem_limit_bytes=VMEM_LIMIT)

    def swap(array, offset):
        return lax.ppermute(array, "expert", [(i, i ^ offset) for i in range(devices)])

    def after(arrays, done):
        return lax.optimization_barrier(tuple(arrays) + tuple(done))[: len(arrays)]

    hid_rows = hidden_saved.reshape(tokens * TOPK, hidden)
    sib_rows = swap(hid_rows, 1)
    dy_z2, dy_z1, dy_x = swap(grad_out, 8), swap(grad_out, 4), swap(grad_out, 2)
    meta, factors = pl.pallas_call(
        functools.partial(norm_kernel, devices),
        out_shape=(
            jax.ShapeDtypeStruct((2 * examples, pairs), jnp.float32),
            jax.ShapeDtypeStruct((1, examples), jnp.float32),
        ),
        compiler_params=pltpu.CompilerParams(vmem_limit_bytes=54 * 1024 * 1024),
        name="norms",
    )(grad_out, hid_rows, expert_ids.T, gate_codes.T, clip_bound.reshape(1, examples))
    sib_meta = swap(meta, 1)
    slots = pl.pallas_call(
        functools.partial(build_kernel, chips),
        out_shape=[jax.ShapeDtypeStruct((2 * tokens, hidden), jnp.bfloat16)] * chips,
        in_specs=[pl.BlockSpec(memory_space=pltpu.SMEM)] + [pl.BlockSpec(memory_space=pltpu.VMEM)] * 4,
        compiler_params=params,
        name="build",
    )(me.astype(jnp.int32).reshape(1), hid_rows, sib_rows, meta, sib_meta)
    slots = list(slots)
    slots[1] = swap(slots[1], 2)
    first = (dy_z2, dy_z1, dy_x, slots[1])

    near = jnp.concatenate([grad_out, dy_z1, dy_x, dy_z2])
    both = jnp.concatenate([dy_z1, dy_z2])
    slot4, slot6, slot3, dy_z2b, both, near = after((slots[4], slots[6], slots[3], dy_z2, both, near), first)
    slots[4], slots[6], slots[3] = swap(slot4, 8), swap(slot6, 12), swap(slot3, 6)
    dy_z3, dy_xz, sib_near = swap(dy_z2b, 4), swap(both, 2), swap(near, 1)
    second = (slots[4], slots[6], slots[3], dy_z3, dy_xz, sib_near)

    far = jnp.concatenate([dy_z3, dy_xz])
    t = tokens
    slot5, slot7, slot2, dy_z3b, far = after((slots[5], slots[7], slots[2], dy_z3, far), second)
    dy_xz3, sib_far = swap(dy_z3b, 2), swap(far, 1)
    where = {
        0: [(grad_out, 0, t), (sib_near, 0, t)],
        1: [(dy_x, 0, t), (sib_near, 2 * t, t)],
        2: [(dy_z1, 0, t), (sib_near, t, t)],
        3: [(dy_xz, 0, t), (sib_far, t, t)],
        4: [(dy_z2, 0, t), (sib_near, 3 * t, t)],
        5: [(dy_xz, t, t), (sib_far, 2 * t, t)],
        6: [(dy_z3, 0, t), (sib_far, 0, t)],
    }
    slots[5], slots[7], slots[2] = swap(slot5, 10), swap(slot7, 14), swap(slot2, 4)
    third = (slots[5], slots[7], slots[2], dy_xz3, sib_far)
    total = product((0, 1, 4, 3, 6), slots, where, True)
    sib_last = swap(after((dy_xz3,), third + (total,))[0], 1)
    where[7] = [(dy_xz3, 0, t), (sib_last, 0, t)]
    rest = [j for j in (3, 6, 5, 2, 7) if j not in (0, 1, 4, 3, 6)]
    summed = product(rest, slots, where, False, total)
    return (summed[None], factors.reshape(examples))


def solution(mesh):
    def per_device(hidden_saved, grad_out, expert_ids, gate_codes, clip_bound):
        devices = mesh.shape["expert"]
        tokens = grad_out.shape[0]
        dense = (
            mesh.shape["dp"] == 1
            and devices == 16
            and 2 * tokens * TOPK // devices >= tokens
        )
        run = per_device_dense if dense else per_device_sparse
        return run(hidden_saved, grad_out, expert_ids, gate_codes, clip_bound)

    return jax.shard_map(
        per_device,
        mesh=mesh,
        in_specs=(
            P(("groups", "expert", "dp"), None, None),
            P(("groups", "expert", "dp"), None),
            P(("groups", "expert", "dp"), None),
            P(("groups", "expert", "dp"), None),
            P(("groups", "expert", "dp")),
        ),
        out_specs=(P(("groups", "expert"), "dp", None), P(("groups", "expert", "dp"))),
        check_vma=False,
    )
```

```python
import functools

import jax
import jax.numpy as jnp
from jax import lax
from jax.experimental import pallas as pl
from jax.experimental.pallas import tpu as pltpu
from jax.sharding import PartitionSpec as P

TOPK = 8
EXLEN = 32
VMEM_LIMIT = 16 * 1024 * 1024
PRODUCT_LIMIT = 32 * 1024 * 1024
LATE_BLOCK = 1024
HIGHEST = lax.Precision.HIGHEST


def per_device_sparse(hidden_saved, grad_out, expert_ids, gate_codes, clip_bound):
    experts = lax.axis_size("expert")
    tokens_dev = grad_out.shape[0]
    width = grad_out.shape[1]
    hidden_width = hidden_saved.shape[2]
    examples_dev = clip_bound.shape[0]
    count_pairs = tokens_dev * TOPK
    capacity = min(tokens_dev, 2 * tokens_dev * TOPK // experts)
    ids_flat = expert_ids.reshape(count_pairs)
    onehot = (ids_flat[:, None] == jnp.arange(experts, dtype=jnp.int32)[None, :]).astype(jnp.int32)
    slot_ids = jnp.sum(jnp.cumsum(onehot, axis=0) * onehot, axis=1) - 1
    target = ids_flat * capacity + slot_ids
    hid_rows = hidden_saved.reshape(count_pairs, hidden_width)
    h_buffer = jnp.zeros((experts * capacity, hidden_width), jnp.bfloat16).at[target].set(hid_rows)
    h_buffer = h_buffer.reshape(experts, capacity, hidden_width)
    dy_pairs = jnp.repeat(grad_out, TOPK, axis=0)
    dy_buffer = jnp.zeros((experts * capacity, width), jnp.bfloat16).at[target].set(dy_pairs)
    dy_buffer = dy_buffer.reshape(experts, capacity, width)
    pair_info = jnp.stack(
        [
            gate_codes.reshape(count_pairs),
            jnp.arange(count_pairs, dtype=jnp.int32) // (EXLEN * TOPK),
        ],
        axis=1,
    ).astype(jnp.bfloat16)
    info_buffer = jnp.zeros((experts * capacity, 2), jnp.bfloat16).at[target].set(pair_info)
    info_buffer = info_buffer.reshape(experts, capacity, 2)
    recv_hidden, recv_dy, recv_info = (
        lax.all_to_all(h_buffer, "expert", split_axis=0, concat_axis=0, tiled=True),
        lax.all_to_all(dy_buffer, "expert", split_axis=0, concat_axis=0, tiled=True),
        lax.all_to_all(info_buffer, "expert", split_axis=0, concat_axis=0, tiled=True),
    )
    gate_recv = recv_info[:, :, 0].astype(jnp.float32) / 1024.0
    example_recv = recv_info[:, :, 1].astype(jnp.float32)
    owner_mask = (
        example_recv[:, :, None] == jnp.arange(examples_dev, dtype=jnp.float32)[None, None, :]
    ).astype(jnp.float32)
    hid_gram = jnp.einsum(
        "smh,snh->smn", recv_hidden, recv_hidden, preferred_element_type=jnp.float32
    )
    grad_gram = jnp.einsum("smd,snd->smn", recv_dy, recv_dy, preferred_element_type=jnp.float32)
    weights = hid_gram * grad_gram * gate_recv[:, :, None] * gate_recv[:, None, :]
    partial_value = jnp.sum(jnp.einsum("smn,snx->smx", weights, owner_mask) * owner_mask, axis=1)
    bounds_all = lax.all_gather(clip_bound, "expert", axis=0, tiled=True).reshape(
        experts, examples_dev
    )
    totals = lax.psum(partial_value, "expert")
    factor_all = jnp.minimum(1.0, bounds_all / jnp.sqrt(totals + 1e-06))
    factors = lax.dynamic_index_in_dim(factor_all, lax.axis_index("expert"), 0, keepdims=False)
    pair_scale = jnp.sum(owner_mask * factor_all[:, None, :], axis=2) * gate_recv
    recv_scaled = (pair_scale[:, :, None] * recv_dy.astype(jnp.float32)).astype(jnp.bfloat16)
    summed = lax.psum_scatter(
        lax.dot_general(
            recv_scaled,
            recv_hidden,
            (((0, 1), (0, 1)), ((), ())),
            preferred_element_type=jnp.float32,
        ).astype(jnp.bfloat16),
        "dp",
        scatter_dimension=0,
        tiled=True,
    )
    return (summed[None], factors)


def norm_kernel(experts, dy_ref, hid_ref, ids_ref, gate_ref, bound_ref, meta_ref, factor_ref):
    examples = bound_ref.shape[1]
    tokens = dy_ref.shape[0]
    pairs = EXLEN * TOPK
    spread = (
        lax.broadcasted_iota(jnp.int32, (pairs, EXLEN), 0) // TOPK
        == lax.broadcasted_iota(jnp.int32, (pairs, EXLEN), 1)
    ).astype(jnp.float32)
    token = lax.broadcasted_iota(jnp.int32, (tokens, tokens * TOPK), 0)
    place = lax.broadcasted_iota(jnp.int32, (tokens, tokens * TOPK), 1)
    widen = (token == place // TOPK).astype(jnp.float32).astype(jnp.bfloat16)
    codes = jnp.concatenate([ids_ref[...], gate_ref[...]], axis=0).astype(jnp.float32).astype(jnp.bfloat16)
    wide = jnp.dot(codes, widen, preferred_element_type=jnp.float32)
    rank = lax.broadcasted_iota(jnp.int32, wide.shape, 0)
    own = rank % TOPK == lax.broadcasted_iota(jnp.int32, wide.shape, 1) % TOPK
    wide = jnp.where(own, wide, 0.0)
    ids_all = jnp.sum(wide[:TOPK], axis=0, keepdims=True)
    gate_all = jnp.sum(wide[TOPK:], axis=0, keepdims=True) / 1024.0
    factor_row = jnp.zeros((1, examples), jnp.float32)
    for x in range(examples):
        ids_row = ids_all[:, x * pairs : (x + 1) * pairs]
        gate_row = gate_all[:, x * pairs : (x + 1) * pairs]
        hid = hid_ref[x * pairs : (x + 1) * pairs, :]
        dy = dy_ref[x * EXLEN : (x + 1) * EXLEN, :]
        hid_gram = lax.dot_general(hid, hid, (((1,), (1,)), ((), ())), preferred_element_type=jnp.float32)
        dy_gram = lax.dot_general(dy, dy, (((1,), (1,)), ((), ())), preferred_element_type=jnp.float32)
        half = jnp.dot(spread, dy_gram, precision=HIGHEST, preferred_element_type=jnp.float32)
        pair_gram = lax.dot_general(
            half, spread, (((1,), (1,)), ((), ())), precision=HIGHEST, preferred_element_type=jnp.float32
        )
        name = lax.broadcasted_iota(jnp.int32, (experts, pairs), 0).astype(jnp.float32)
        onehot = (name == ids_row).astype(jnp.float32)
        same = lax.dot_general(onehot, onehot, (((0,), (0,)), ((), ())), preferred_element_type=jnp.float32)
        weights = hid_gram * pair_gram * same
        sums = jnp.dot(gate_row, weights, precision=HIGHEST, preferred_element_type=jnp.float32)
        norm = jnp.sum(sums * gate_row, axis=1, keepdims=True)
        factor = jnp.minimum(1.0, bound_ref[:, x : x + 1] / jnp.sqrt(norm + 1e-06))
        lane = lax.broadcasted_iota(jnp.int32, (1, examples), 1)
        factor_row = jnp.where(lane == x, factor, factor_row)
        meta_ref[x : x + 1, :] = factor * gate_row
        meta_ref[examples + x : examples + x + 1, :] = ids_row
    factor_ref[...] = factor_row


def build_kernel(chips, place_ref, own_ref, sib_ref, own_meta_ref, sib_meta_ref, *out_refs):
    examples = own_meta_ref.shape[0] // 2
    pairs = EXLEN * TOPK
    rows = chips * EXLEN
    me = place_ref[0]
    row = lax.broadcasted_iota(jnp.int32, (rows, pairs), 0)
    lane = lax.broadcasted_iota(jnp.int32, (rows, pairs), 1)
    same_token = (row % EXLEN) == (lane // TOPK)
    expert = (lax.bitwise_xor(row // EXLEN, me // 2) * 2 + me % 2).astype(jnp.float32)
    for side, (hid_ref, meta_ref) in enumerate(((own_ref, own_meta_ref), (sib_ref, sib_meta_ref))):
        for x in range(examples):
            hit = same_token & (meta_ref[examples + x : examples + x + 1, :] == expert)
            scale = jnp.sum(jnp.where(hit, meta_ref[x : x + 1, :], 0.0), axis=1, keepdims=True)
            picked = jnp.dot(
                hit.astype(jnp.float32).astype(jnp.bfloat16),
                hid_ref[x * pairs : (x + 1) * pairs, :],
                preferred_element_type=jnp.float32,
            )
            message = (picked * scale).astype(jnp.bfloat16)
            start = (side * examples + x) * EXLEN
            for j in range(chips):
                out_refs[j][start : start + EXLEN, :] = message[j * EXLEN : (j + 1) * EXLEN, :]


def product_kernel(places, block, has_total, *refs):
    m = len(places)
    n = len(refs) - m - 3 - has_total
    dy_refs, hid_refs, (out_ref, out_tiles, out_sems) = refs[:n], refs[n : n + m], refs[n + m + has_total :]
    chunks = out_ref.shape[0] // block

    def out_copy(c):
        return pltpu.make_async_copy(
            out_tiles.at[c % 2], out_ref.at[pl.ds(c * block, block), :], out_sems.at[c % 2]
        )

    for c in range(chunks):
        if c >= 2:
            out_copy(c - 2).wait()
        columns = slice(c * block, (c + 1) * block)
        dy = jnp.concatenate(
            [dy_refs[k][begin : begin + rows, columns] for sides in places for k, begin, rows in sides], axis=0
        )
        hid = jnp.concatenate([hid_ref[...] for hid_ref in hid_refs], axis=0)
        value = lax.dot_general(dy, hid, (((0,), (0,)), ((), ())), preferred_element_type=jnp.float32)
        if has_total:
            value = value + refs[n + m][columns, :]
        out_tiles[c % 2] = value.astype(out_tiles.dtype)
        out_copy(c).start()
    for c in range(max(chunks - 2, 0), chunks):
        out_copy(c).wait()


def early_kernel(places, block, *refs):
    m = len(places)
    n = len(refs) - m - 1
    dy_refs, hid_refs, out_ref = refs[:n], refs[n : n + m], refs[n + m]
    for c in range(out_ref.shape[0] // block):
        columns = slice(c * block, (c + 1) * block)
        dy = jnp.concatenate(
            [dy_refs[k][begin : begin + rows, columns] for sides in places for k, begin, rows in sides], axis=0
        )
        hid = jnp.concatenate([hid_ref[...] for hid_ref in hid_refs], axis=0)
        out_ref[columns, :] = lax.dot_general(dy, hid, (((0,), (0,)), ((), ())), preferred_element_type=jnp.float32)


def product(offsets, slots, where, early, total=None):
    arrays, places = [], []
    for j in offsets:
        sides = []
        for array, begin, rows in where[j]:
            known = [k for k, other in enumerate(arrays) if other is array]
            if not known:
                arrays.append(array)
            sides.append((known[0] if known else len(arrays) - 1, begin, rows))
        places.append(sides)
    width, hidden = arrays[0].shape[1], slots[0].shape[1]
    operands = arrays + [slots[j] for j in offsets] + ([] if total is None else [total])
    if early:
        block = min(width, 512)
        kernel = functools.partial(early_kernel, places, block)
        out_space, scratch = pltpu.VMEM, ()
    else:
        block = min(width, LATE_BLOCK)
        kernel = functools.partial(product_kernel, places, block, int(total is not None))
        out_space = pl.ANY
        scratch = (pltpu.VMEM((2, block, hidden), jnp.bfloat16), pltpu.SemaphoreType.DMA((2,)))
    return pl.pallas_call(
        kernel,
        out_shape=jax.ShapeDtypeStruct((width, hidden), jnp.float32 if early else jnp.bfloat16),
        in_specs=[pl.BlockSpec(memory_space=pltpu.VMEM)] * len(operands),
        out_specs=pl.BlockSpec(memory_space=out_space),
        scratch_shapes=scratch,
        compiler_params=pltpu.CompilerParams(vmem_limit_bytes=PRODUCT_LIMIT),
        cost_estimate=pl.CostEstimate(
            flops=2 * width * hidden * sum(slots[j].shape[0] for j in offsets),
            bytes_accessed=2 * width * hidden,
            transcendentals=0,
        ),
        name="early_product" if early else "product",
    )(*operands)


def per_device_dense(hidden_saved, grad_out, expert_ids, gate_codes, clip_bound):
    devices = lax.axis_size("expert")
    chips = devices // 2
    tokens, width = grad_out.shape
    hidden = hidden_saved.shape[2]
    examples = clip_bound.shape[0]
    pairs = EXLEN * TOPK
    me = lax.axis_index("expert")
    params = pltpu.CompilerParams(vmem_limit_bytes=VMEM_LIMIT)

    def swap(array, offset):
        return lax.ppermute(array, "expert", [(i, i ^ offset) for i in range(devices)])

    def after(arrays, done):
        return lax.optimization_barrier(tuple(arrays) + tuple(done))[: len(arrays)]

    hid_rows = hidden_saved.reshape(tokens * TOPK, hidden)
    sib_rows = swap(hid_rows, 1)
    dy_z2, dy_z1, dy_x = swap(grad_out, 8), swap(grad_out, 4), swap(grad_out, 2)
    meta, factors = pl.pallas_call(
        functools.partial(norm_kernel, devices),
        out_shape=(
            jax.ShapeDtypeStruct((2 * examples, pairs), jnp.float32),
            jax.ShapeDtypeStruct((1, examples), jnp.float32),
        ),
        compiler_params=pltpu.CompilerParams(vmem_limit_bytes=54 * 1024 * 1024),
        name="norms",
    )(grad_out, hid_rows, expert_ids.T, gate_codes.T, clip_bound.reshape(1, examples))
    sib_meta = swap(meta, 1)
    slots = pl.pallas_call(
        functools.partial(build_kernel, chips),
        out_shape=[jax.ShapeDtypeStruct((2 * tokens, hidden), jnp.bfloat16)] * chips,
        in_specs=[pl.BlockSpec(memory_space=pltpu.SMEM)] + [pl.BlockSpec(memory_space=pltpu.VMEM)] * 4,
        compiler_params=params,
        name="build",
    )(me.astype(jnp.int32).reshape(1), hid_rows, sib_rows, meta, sib_meta)
    slots = list(slots)
    slots[1] = swap(slots[1], 2)
    first = (dy_z2, dy_z1, dy_x, slots[1])

    both = jnp.concatenate([dy_z1, dy_z2])
    slot4, slot6, slot3, dy_z2b, both = after((slots[5], slots[6], slots[2], dy_z2, both), first)
    slots[5], slots[6], slots[2] = swap(slot4, 10), swap(slot6, 12), swap(slot3, 4)
    dy_z3, dy_xz = swap(dy_z2b, 4), swap(both, 2)
    second = (slots[5], slots[6], slots[2], dy_z3, dy_xz)

    far = jnp.concatenate([grad_out, dy_z1, dy_x, dy_z2, dy_z3, dy_xz])
    t = tokens
    slot5, slot7, slot2, dy_z3b, far = after((slots[4], slots[7], slots[3], dy_z3, far), second)
    dy_xz3, sib_far = swap(dy_z3b, 2), swap(far, 1)
    where = {
        0: [(grad_out, 0, t), (sib_far, 0, t)],
        1: [(dy_x, 0, t), (sib_far, 2 * t, t)],
        2: [(dy_z1, 0, t), (sib_far, t, t)],
        3: [(dy_xz, 0, t), (sib_far, 5 * t, t)],
        4: [(dy_z2, 0, t), (sib_far, 3 * t, t)],
        5: [(dy_xz, t, t), (sib_far, 6 * t, t)],
        6: [(dy_z3, 0, t), (sib_far, 4 * t, t)],
    }
    slots[4], slots[7], slots[3] = swap(slot5, 8), swap(slot7, 14), swap(slot2, 6)
    third = (slots[4], slots[7], slots[3], dy_xz3, sib_far)
    total = product((0, 1, 5, 6, 2), slots, where, True)
    sib_last = swap(after((dy_xz3,), third + (total,))[0], 1)
    where[7] = [(dy_xz3, 0, t), (sib_last, 0, t)]
    rest = [4, 7, 3]
    summed = product(rest, slots, where, False, total)
    return (summed[None], factors.reshape(examples))


def solution(mesh):
    def per_device(hidden_saved, grad_out, expert_ids, gate_codes, clip_bound):
        devices = mesh.shape["expert"]
        tokens = grad_out.shape[0]
        dense = (
            mesh.shape["dp"] == 1
            and devices == 16
            and 2 * tokens * TOPK // devices >= tokens
        )
        run = per_device_dense if dense else per_device_sparse
        return run(hidden_saved, grad_out, expert_ids, gate_codes, clip_bound)

    return jax.shard_map(
        per_device,
        mesh=mesh,
        in_specs=(
            P(("groups", "expert", "dp"), None, None),
            P(("groups", "expert", "dp"), None),
            P(("groups", "expert", "dp"), None),
            P(("groups", "expert", "dp"), None),
            P(("groups", "expert", "dp")),
        ),
        out_specs=(P(("groups", "expert"), "dp", None), P(("groups", "expert", "dp"))),
        check_vma=False,
    )
```

```python
import functools

import jax
import jax.numpy as jnp
from jax import lax
from jax.experimental import pallas as pl
from jax.experimental.pallas import tpu as pltpu
from jax.sharding import PartitionSpec as P

TOPK = 8
EXLEN = 32
VMEM_LIMIT = 16 * 1024 * 1024
PRODUCT_LIMIT = 32 * 1024 * 1024
LATE_BLOCK = 1024


def per_device_sparse(hidden_saved, grad_out, expert_ids, gate_codes, clip_bound):
    experts = lax.axis_size("expert")
    tokens_dev = grad_out.shape[0]
    width = grad_out.shape[1]
    hidden_width = hidden_saved.shape[2]
    examples_dev = clip_bound.shape[0]
    count_pairs = tokens_dev * TOPK
    capacity = min(tokens_dev, 2 * tokens_dev * TOPK // experts)
    ids_flat = expert_ids.reshape(count_pairs)
    onehot = (ids_flat[:, None] == jnp.arange(experts, dtype=jnp.int32)[None, :]).astype(jnp.int32)
    slot_ids = jnp.sum(jnp.cumsum(onehot, axis=0) * onehot, axis=1) - 1
    target = ids_flat * capacity + slot_ids
    hid_rows = hidden_saved.reshape(count_pairs, hidden_width)
    h_buffer = jnp.zeros((experts * capacity, hidden_width), jnp.bfloat16).at[target].set(hid_rows)
    h_buffer = h_buffer.reshape(experts, capacity, hidden_width)
    dy_pairs = jnp.repeat(grad_out, TOPK, axis=0)
    dy_buffer = jnp.zeros((experts * capacity, width), jnp.bfloat16).at[target].set(dy_pairs)
    dy_buffer = dy_buffer.reshape(experts, capacity, width)
    pair_info = jnp.stack(
        [
            gate_codes.reshape(count_pairs),
            jnp.arange(count_pairs, dtype=jnp.int32) // (EXLEN * TOPK),
        ],
        axis=1,
    ).astype(jnp.bfloat16)
    info_buffer = jnp.zeros((experts * capacity, 2), jnp.bfloat16).at[target].set(pair_info)
    info_buffer = info_buffer.reshape(experts, capacity, 2)
    recv_hidden, recv_dy, recv_info = (
        lax.all_to_all(h_buffer, "expert", split_axis=0, concat_axis=0, tiled=True),
        lax.all_to_all(dy_buffer, "expert", split_axis=0, concat_axis=0, tiled=True),
        lax.all_to_all(info_buffer, "expert", split_axis=0, concat_axis=0, tiled=True),
    )
    gate_recv = recv_info[:, :, 0].astype(jnp.float32) / 1024.0
    example_recv = recv_info[:, :, 1].astype(jnp.float32)
    owner_mask = (
        example_recv[:, :, None] == jnp.arange(examples_dev, dtype=jnp.float32)[None, None, :]
    ).astype(jnp.float32)
    hid_gram = jnp.einsum(
        "smh,snh->smn", recv_hidden, recv_hidden, preferred_element_type=jnp.float32
    )
    grad_gram = jnp.einsum("smd,snd->smn", recv_dy, recv_dy, preferred_element_type=jnp.float32)
    weights = hid_gram * grad_gram * gate_recv[:, :, None] * gate_recv[:, None, :]
    partial_value = jnp.sum(jnp.einsum("smn,snx->smx", weights, owner_mask) * owner_mask, axis=1)
    bounds_all = lax.all_gather(clip_bound, "expert", axis=0, tiled=True).reshape(
        experts, examples_dev
    )
    totals = lax.psum(partial_value, "expert")
    factor_all = jnp.minimum(1.0, bounds_all / jnp.sqrt(totals + 1e-06))
    factors = lax.dynamic_index_in_dim(factor_all, lax.axis_index("expert"), 0, keepdims=False)
    pair_scale = jnp.sum(owner_mask * factor_all[:, None, :], axis=2) * gate_recv
    recv_scaled = (pair_scale[:, :, None] * recv_dy.astype(jnp.float32)).astype(jnp.bfloat16)
    summed = lax.psum_scatter(
        lax.dot_general(
            recv_scaled,
            recv_hidden,
            (((0, 1), (0, 1)), ((), ())),
            preferred_element_type=jnp.float32,
        ).astype(jnp.bfloat16),
        "dp",
        scatter_dimension=0,
        tiled=True,
    )
    return (summed[None], factors)


def three_terms(value, axis):
    first = value.astype(jnp.bfloat16)
    rest = value - first.astype(jnp.float32)
    second = rest.astype(jnp.bfloat16)
    third = (rest - second.astype(jnp.float32)).astype(jnp.bfloat16)
    return jnp.concatenate([first, second, third], axis=axis)


def norm_kernel(experts, dy_ref, hid_ref, ids_ref, gate_ref, bound_ref, meta_ref, factor_ref):
    examples = bound_ref.shape[1]
    tokens = dy_ref.shape[0]
    pairs = EXLEN * TOPK
    spread = jnp.where(
        lax.broadcasted_iota(jnp.int32, (pairs, 3 * EXLEN), 0) // TOPK
        == lax.broadcasted_iota(jnp.int32, (pairs, 3 * EXLEN), 1) % EXLEN,
        1.0,
        0.0,
    ).astype(jnp.bfloat16)
    token = lax.broadcasted_iota(jnp.int32, (tokens, tokens * TOPK), 0)
    place = lax.broadcasted_iota(jnp.int32, (tokens, tokens * TOPK), 1)
    widen = (token == place // TOPK).astype(jnp.float32).astype(jnp.bfloat16)
    codes = jnp.concatenate([ids_ref[...], gate_ref[...]], axis=0).astype(jnp.float32).astype(jnp.bfloat16)
    wide = jnp.dot(codes, widen, preferred_element_type=jnp.float32)
    rank = lax.broadcasted_iota(jnp.int32, wide.shape, 0)
    own = rank % TOPK == lax.broadcasted_iota(jnp.int32, wide.shape, 1) % TOPK
    wide = jnp.where(own, wide, 0.0)
    ids_all = jnp.sum(wide[:TOPK], axis=0, keepdims=True)
    gate_all = jnp.sum(wide[TOPK:], axis=0, keepdims=True) / 1024.0
    name = lax.broadcasted_iota(jnp.int32, (experts, pairs), 0).astype(jnp.float32)
    lane = lax.broadcasted_iota(jnp.int32, (1, examples), 1)
    gates, weights, halves, hid_grams = [], [], [], []
    for x in range(examples):
        dy = dy_ref[x * EXLEN : (x + 1) * EXLEN, :]
        dy_gram = lax.dot_general(dy, dy, (((1,), (1,)), ((), ())), preferred_element_type=jnp.float32)
        halves.append(jnp.dot(spread, three_terms(dy_gram, 0), preferred_element_type=jnp.float32))
    for x in range(examples):
        ids_row = ids_all[:, x * pairs : (x + 1) * pairs]
        gate_row = gate_all[:, x * pairs : (x + 1) * pairs]
        named = jnp.where(name == ids_row, gate_row, 0.0).astype(jnp.bfloat16)
        weights.append(
            lax.dot_general(named, named, (((0,), (0,)), ((), ())), preferred_element_type=jnp.float32)
        )
        gates.append(gate_row)
        meta_ref[examples + x : examples + x + 1, :] = ids_row
    for x in range(examples):
        hid = hid_ref[x * pairs : (x + 1) * pairs, :]
        hid_grams.append(
            lax.dot_general(hid, hid, (((1,), (1,)), ((), ())), preferred_element_type=jnp.float32)
        )
    factor_row = jnp.zeros((1, examples), jnp.float32)
    for x in range(examples):
        pair_gram = lax.dot_general(
            three_terms(halves[x], 1), spread, (((1,), (1,)), ((), ())), preferred_element_type=jnp.float32
        )
        products = hid_grams[x] * pair_gram * weights[x]
        norm = jnp.sum(jnp.sum(products, axis=0, keepdims=True), axis=1, keepdims=True)
        factor = jnp.minimum(1.0, bound_ref[:, x : x + 1] / jnp.sqrt(norm + 1e-06))
        factor_row = jnp.where(lane == x, factor, factor_row)
        meta_ref[x : x + 1, :] = factor * gates[x]
    factor_ref[...] = factor_row


def build_kernel(chips, place_ref, own_ref, sib_ref, own_meta_ref, sib_meta_ref, *out_refs):
    examples = own_meta_ref.shape[0] // 2
    pairs = EXLEN * TOPK
    rows = chips * EXLEN
    me = place_ref[0]
    row = lax.broadcasted_iota(jnp.int32, (rows, pairs), 0)
    lane = lax.broadcasted_iota(jnp.int32, (rows, pairs), 1)
    same_token = (row % EXLEN) == (lane // TOPK)
    expert = (lax.bitwise_xor(row // EXLEN, me // 2) * 2 + me % 2).astype(jnp.float32)
    for side, (hid_ref, meta_ref) in enumerate(((own_ref, own_meta_ref), (sib_ref, sib_meta_ref))):
        for x in range(examples):
            hit = same_token & (meta_ref[examples + x : examples + x + 1, :] == expert)
            scale = jnp.sum(jnp.where(hit, meta_ref[x : x + 1, :], 0.0), axis=1, keepdims=True)
            picked = jnp.dot(
                hit.astype(jnp.float32).astype(jnp.bfloat16),
                hid_ref[x * pairs : (x + 1) * pairs, :],
                preferred_element_type=jnp.float32,
            )
            message = (picked * scale).astype(jnp.bfloat16)
            start = (side * examples + x) * EXLEN
            for j in range(chips):
                out_refs[j][start : start + EXLEN, :] = message[j * EXLEN : (j + 1) * EXLEN, :]


def product_kernel(places, block, has_total, *refs):
    m = len(places)
    n = len(refs) - m - 3 - has_total
    dy_refs, hid_refs, (out_ref, out_tiles, out_sems) = refs[:n], refs[n : n + m], refs[n + m + has_total :]
    chunks = out_ref.shape[0] // block

    def out_copy(c):
        return pltpu.make_async_copy(
            out_tiles.at[c % 2], out_ref.at[pl.ds(c * block, block), :], out_sems.at[c % 2]
        )

    for c in range(chunks):
        if c >= 2:
            out_copy(c - 2).wait()
        columns = slice(c * block, (c + 1) * block)
        dy = jnp.concatenate(
            [dy_refs[k][begin : begin + rows, columns] for sides in places for k, begin, rows in sides], axis=0
        )
        hid = jnp.concatenate([hid_ref[...] for hid_ref in hid_refs], axis=0)
        value = lax.dot_general(dy, hid, (((0,), (0,)), ((), ())), preferred_element_type=jnp.float32)
        if has_total:
            value = value + refs[n + m][columns, :]
        out_tiles[c % 2] = value.astype(out_tiles.dtype)
        out_copy(c).start()
    for c in range(max(chunks - 2, 0), chunks):
        out_copy(c).wait()


def early_kernel(places, block, *refs):
    m = len(places)
    n = len(refs) - m - 1
    dy_refs, hid_refs, out_ref = refs[:n], refs[n : n + m], refs[n + m]
    for c in range(out_ref.shape[0] // block):
        columns = slice(c * block, (c + 1) * block)
        dy = jnp.concatenate(
            [dy_refs[k][begin : begin + rows, columns] for sides in places for k, begin, rows in sides], axis=0
        )
        hid = jnp.concatenate([hid_ref[...] for hid_ref in hid_refs], axis=0)
        out_ref[columns, :] = lax.dot_general(dy, hid, (((0,), (0,)), ((), ())), preferred_element_type=jnp.float32)


def product(offsets, slots, where, early, total=None):
    arrays, places = [], []
    for j in offsets:
        sides = []
        for array, begin, rows in where[j]:
            known = [k for k, other in enumerate(arrays) if other is array]
            if not known:
                arrays.append(array)
            sides.append((known[0] if known else len(arrays) - 1, begin, rows))
        places.append(sides)
    width, hidden = arrays[0].shape[1], slots[0].shape[1]
    operands = arrays + [slots[j] for j in offsets] + ([] if total is None else [total])
    if early:
        block = min(width, 512)
        kernel = functools.partial(early_kernel, places, block)
        out_space, scratch = pltpu.VMEM, ()
    else:
        block = min(width, LATE_BLOCK)
        kernel = functools.partial(product_kernel, places, block, int(total is not None))
        out_space = pl.ANY
        scratch = (pltpu.VMEM((2, block, hidden), jnp.bfloat16), pltpu.SemaphoreType.DMA((2,)))
    return pl.pallas_call(
        kernel,
        out_shape=jax.ShapeDtypeStruct((width, hidden), jnp.float32 if early else jnp.bfloat16),
        in_specs=[pl.BlockSpec(memory_space=pltpu.VMEM)] * len(operands),
        out_specs=pl.BlockSpec(memory_space=out_space),
        scratch_shapes=scratch,
        compiler_params=pltpu.CompilerParams(vmem_limit_bytes=PRODUCT_LIMIT),
        cost_estimate=pl.CostEstimate(
            flops=2 * width * hidden * sum(slots[j].shape[0] for j in offsets),
            bytes_accessed=2 * width * hidden,
            transcendentals=0,
        ),
        name="early_product" if early else "product",
    )(*operands)


def per_device_dense(hidden_saved, grad_out, expert_ids, gate_codes, clip_bound):
    devices = lax.axis_size("expert")
    chips = devices // 2
    tokens, width = grad_out.shape
    hidden = hidden_saved.shape[2]
    examples = clip_bound.shape[0]
    pairs = EXLEN * TOPK
    me = lax.axis_index("expert")
    params = pltpu.CompilerParams(vmem_limit_bytes=VMEM_LIMIT)

    def swap(array, offset):
        return lax.ppermute(array, "expert", [(i, i ^ offset) for i in range(devices)])

    def after(arrays, done):
        return lax.optimization_barrier(tuple(arrays) + tuple(done))[: len(arrays)]

    hid_rows = hidden_saved.reshape(tokens * TOPK, hidden)
    sib_rows = swap(hid_rows, 1)
    dy_z2, dy_z1, dy_x = swap(grad_out, 8), swap(grad_out, 4), swap(grad_out, 2)
    meta, factors = pl.pallas_call(
        functools.partial(norm_kernel, devices),
        out_shape=(
            jax.ShapeDtypeStruct((2 * examples, pairs), jnp.float32),
            jax.ShapeDtypeStruct((1, examples), jnp.float32),
        ),
        compiler_params=pltpu.CompilerParams(vmem_limit_bytes=54 * 1024 * 1024),
        name="norms",
    )(grad_out, hid_rows, expert_ids.T, gate_codes.T, clip_bound.reshape(1, examples))
    sib_meta = swap(meta, 1)
    slots = pl.pallas_call(
        functools.partial(build_kernel, chips),
        out_shape=[jax.ShapeDtypeStruct((2 * tokens, hidden), jnp.bfloat16)] * chips,
        in_specs=[pl.BlockSpec(memory_space=pltpu.SMEM)] + [pl.BlockSpec(memory_space=pltpu.VMEM)] * 4,
        compiler_params=params,
        name="build",
    )(me.astype(jnp.int32).reshape(1), hid_rows, sib_rows, meta, sib_meta)
    slots = list(slots)
    slots[1] = swap(slots[1], 2)
    first = (dy_z2, dy_z1, dy_x, slots[1])

    both = jnp.concatenate([dy_z1, dy_z2])
    slot4, slot6, slot3, dy_z2b, both = after((slots[5], slots[6], slots[2], dy_z2, both), first)
    slots[5], slots[6], slots[2] = swap(slot4, 10), swap(slot6, 12), swap(slot3, 4)
    dy_z3, dy_xz = swap(dy_z2b, 4), swap(both, 2)
    second = (slots[5], slots[6], slots[2], dy_z3, dy_xz)

    far = jnp.concatenate([grad_out, dy_z1, dy_x, dy_z2, dy_z3, dy_xz])
    t = tokens
    slot5, slot7, slot2, dy_z3b, far = after((slots[4], slots[7], slots[3], dy_z3, far), second)
    dy_xz3, sib_far = swap(dy_z3b, 2), swap(far, 1)
    where = {
        0: [(grad_out, 0, t), (sib_far, 0, t)],
        1: [(dy_x, 0, t), (sib_far, 2 * t, t)],
        2: [(dy_z1, 0, t), (sib_far, t, t)],
        3: [(dy_xz, 0, t), (sib_far, 5 * t, t)],
        4: [(dy_z2, 0, t), (sib_far, 3 * t, t)],
        5: [(dy_xz, t, t), (sib_far, 6 * t, t)],
        6: [(dy_z3, 0, t), (sib_far, 4 * t, t)],
    }
    slots[4], slots[7], slots[3] = swap(slot5, 8), swap(slot7, 14), swap(slot2, 6)
    third = (slots[4], slots[7], slots[3], dy_xz3, sib_far)
    total = product((0, 1, 5, 6, 2), slots, where, True)
    sib_last = swap(after((dy_xz3,), third + (total,))[0], 1)
    where[7] = [(dy_xz3, 0, t), (sib_last, 0, t)]
    rest = [4, 7, 3]
    summed = product(rest, slots, where, False, total)
    return (summed[None], factors.reshape(examples))


def solution(mesh):
    def per_device(hidden_saved, grad_out, expert_ids, gate_codes, clip_bound):
        devices = mesh.shape["expert"]
        tokens = grad_out.shape[0]
        dense = (
            mesh.shape["dp"] == 1
            and devices == 16
            and 2 * tokens * TOPK // devices >= tokens
        )
        run = per_device_dense if dense else per_device_sparse
        return run(hidden_saved, grad_out, expert_ids, gate_codes, clip_bound)

    return jax.shard_map(
        per_device,
        mesh=mesh,
        in_specs=(
            P(("groups", "expert", "dp"), None, None),
            P(("groups", "expert", "dp"), None),
            P(("groups", "expert", "dp"), None),
            P(("groups", "expert", "dp"), None),
            P(("groups", "expert", "dp")),
        ),
        out_specs=(P(("groups", "expert"), "dp", None), P(("groups", "expert", "dp"))),
        check_vma=False,
    )
```
